128 devices in a mesh: tsec: 2 (over x_lo), dp: 32 (over y, z, core), rep: 2 (over x_hi).
Axes of the slice: x: 4 (x_hi: 2, x_lo: 2; x = x_hi * 2 + x_lo), y: 4, z: 4, core: 2. Of those that a mesh axis runs over, the one named last changes fastest.
Arguments:
- student: bfloat16 [131072, 1280], P(('dp', 'rep')), may hold values from -700 to 700
- dino_feat: bfloat16 [131072, 1536], P(('dp', 'rep'), 'tsec'), may hold values from -80 to 80
- siglip_feat: bfloat16 [131072, 1152], P(('dp', 'rep'), 'tsec'), may hold values from -80 to 80
- dino_weight: bfloat16 [1280, 1536], P(None, 'tsec'), may hold values from -0.15625 to 0.15625
- siglip_weight: bfloat16 [1280, 1152], P(None, 'tsec'), may hold values from -0.15625 to 0.15625
- send_index: int32 [131072], P(('dp', 'rep')), may hold values from 0 to 4095, as said below
- recv_index: int32 [131072], P(('dp', 'rep')), may hold values from 0 to 4095, as said below
Outputs:
- feature_grad: bfloat16 [131072, 1280], P(('dp', 'rep'))
- dino_wgrad: float32 [1280, 1536], P('dp', 'tsec')
- siglip_wgrad: float32 [1280, 1152], P('dp', 'tsec')
The draws below stay inside these ranges and needn't reach their ends.
Inputs may be any that keep to these rules, and one draw needn't show every extreme that they name: `send_index`: on each teacher shard the 2048 values are distinct; towards each student shard a teacher shard uses exactly the slots 0 to c - 1 for some count c, and every teacher shard sends 64 rows to some student shard. All teacher shards send the same multiset of counts, some of them zero. `recv_index`: on each student shard the 2048 values are distinct and are exactly the (teacher shard, slot) pairs sent to that shard, so that every student row is paired with one teacher row and every teacher row with one student row.
All inputs are finite; a program needn't handle non-finite values.
Results may differ from the reference program's by a relative error of at most 0.018.
Values may be sent and summed in bfloat16 or wider, within the bound.
A program may use at most 128 MiB of HBM per device.

```python
import math
import jax
import jax.numpy as jnp
from jax import lax

D = 1280
E1 = 1536
E2 = 1152
TOK_DEV = 2048
CAP = 64
TOKENS = 131072
N_TSEC = 2
N_DP = 32
N_REP = 2


def spread_rows(count_row, positions):
    running_end = jnp.cumsum(count_row)
    which_block = jnp.searchsorted(running_end, positions, side='right').astype(jnp.int32)
    offset = positions - (running_end[which_block] - count_row[which_block])
    return (which_block, offset.astype(jnp.int32))


def place_rows(subkey, row_values):
    row_perm = jax.random.permutation(subkey, TOK_DEV).astype(jnp.int32)
    return jnp.zeros((TOK_DEV,), jnp.int32).at[row_perm].set(row_values)


def routing_plan(key):
    groups = N_DP * N_REP
    mean_rows = TOK_DEV // groups
    key_extra, key_order, key_shift, key_send, key_recv = jax.random.split(key, 5)
    extra_rows = jax.random.randint(key_extra, (groups // 2,), 0, mean_rows + 1).astype(jnp.int32)
    extra_rows = extra_rows.at[0].set(mean_rows)
    counts = jnp.concatenate([mean_rows + extra_rows, mean_rows - extra_rows]).astype(jnp.int32)
    counts = counts[jax.random.permutation(key_order, groups).astype(jnp.int32)]
    shift_perm = jax.random.permutation(key_shift, groups).astype(jnp.int32)
    lane_ids = jnp.arange(groups, dtype=jnp.int32)
    pairs = counts[(lane_ids[None, :] + shift_perm[:, None]) % groups]
    positions = jnp.arange(TOK_DEV, dtype=jnp.int32)
    dest_group, slot_index = jax.vmap(lambda count_row: spread_rows(count_row, positions))(pairs)
    send_values = dest_group * CAP + slot_index
    sent = jax.vmap(place_rows)(jax.random.split(key_send, groups), send_values)
    source_group, recv_slot = jax.vmap(lambda count_col: spread_rows(count_col, positions))(pairs.T)
    recv_values = source_group * CAP + recv_slot
    received = jax.vmap(place_rows)(jax.random.split(key_recv, groups), recv_values)
    return (sent.reshape(TOKENS), received.reshape(TOKENS))


def draw_send_index(key, part):
    return routing_plan(key)[0]


def draw_recv_index(key, part):
    return routing_plan(key)[1]


def draw_student(key, part):
    key = jax.random.fold_in(key, 11)
    key_base, key_rows, key_cols = jax.random.split(key, 3)
    col_scale = jnp.exp(jax.random.uniform(key_cols, (1, D), minval=0.0, maxval=math.log(10.0)))
    base_draw = jnp.clip(jax.random.normal(key_base, (TOKENS, D)), -4.0, 4.0)
    row_scale = jnp.exp(jax.random.uniform(key_rows, (TOKENS, 1), minval=0.0, maxval=math.log(10.0)))
    return (base_draw * row_scale * col_scale).astype(jnp.bfloat16)


def teacher_columns(subkey, head_width):
    col_ramp = jnp.exp(math.log(3.0) * jnp.arange(head_width, dtype=jnp.float32) / head_width)
    col_noise = jnp.exp(jax.random.uniform(subkey, (1, head_width), minval=math.log(0.5), maxval=math.log(2.0)))
    return col_ramp[None, :] * col_noise


def teacher_rows(subkey):
    return jnp.exp(jax.random.uniform(subkey, (TOKENS, 1), minval=math.log(0.3), maxval=math.log(3.0)))


def draw_dino_feat(key, part):
    key = jax.random.fold_in(key, 21)
    key_base, key_cols, key_rows = jax.random.split(key, 3)
    col_scale = teacher_columns(key_cols, E1)
    row_scale = teacher_rows(key_rows)
    base_draw = jnp.clip(jax.random.normal(key_base, (TOKENS, E1)), -4.0, 4.0)
    return (base_draw * row_scale * col_scale).astype(jnp.bfloat16)


def draw_siglip_feat(key, part):
    key = jax.random.fold_in(key, 22)
    key_base, key_cols, key_rows = jax.random.split(key, 3)
    col_scale = teacher_columns(key_cols, E2)
    row_scale = teacher_rows(key_rows)
    base_draw = jnp.clip(jax.random.normal(key_base, (TOKENS, E2)), -4.0, 4.0)
    return (base_draw * row_scale * col_scale).astype(jnp.bfloat16)


def block_levels(stream_key, dims, shards, low, top_value):
    loudness = 1.0
    for position, shards_of in shards:
        heights = jax.random.uniform(jax.random.fold_in(jax.random.fold_in(stream_key, 6), position), (shards_of,), jnp.float32, low / len(shards), top_value / len(shards))
        loudness = loudness * jnp.repeat(jnp.exp(heights), dims[position] // shards_of).reshape((-1,) + (1,) * (len(dims) - 1 - position))
    return loudness


def bell_draw(rng, dims, scale, most, cuts=(), kind=jnp.bfloat16):
    level = block_levels(rng, dims, cuts, -0.22, 0.18) if cuts else 1.0
    entries = jax.random.normal(rng, dims, jnp.float32) * scale * level
    return jnp.minimum(jnp.maximum(entries, -most), most).astype(kind)


def setup_inputs(seed: int = 0) -> dict:
    key_list = jax.random.split(jax.random.key(seed), 8)
    return {
        "student": draw_student(jax.random.fold_in(key_list[7], 71), 0),
        "dino_feat": draw_dino_feat(jax.random.fold_in(key_list[7], 71), 0),
        "siglip_feat": draw_siglip_feat(jax.random.fold_in(key_list[7], 71), 0),
        "dino_weight": bell_draw(key_list[3], (D, E1), D ** -0.5, 0.15625, ((1, 2),)),
        "siglip_weight": bell_draw(key_list[4], (D, E2), D ** -0.5, 0.15625, ((1, 2),)),
        "send_index": draw_send_index(jax.random.fold_in(key_list[7], 71), 0),
        "recv_index": draw_recv_index(jax.random.fold_in(key_list[7], 71), 0),
    }


norm_eps = 1e-05
length_eps = 1e-06

def back_product(left_op, right_op):
    return lax.dot_general(left_op, right_op, (((1,), (1,)), ((), ())), preferred_element_type=jnp.float32)

def head_delta(output, target, stat_sums, head_width):
    out_sq, tgt_sq, cross = stat_sums
    out_len = jnp.sqrt(out_sq + length_eps)
    tgt_len = jnp.sqrt(tgt_sq + length_eps)
    cosine = cross / (out_len * tgt_len)
    cos_pull = target / (out_len * tgt_len)[:, None] - (cosine / (out_len * out_len))[:, None] * output
    return (jnp.clip(output - target, -1.0, 1.0) - head_width * cos_pull).astype(jnp.bfloat16)

def row_stats(output, target):
    return (lax.optimization_barrier(jnp.sum(output * output, 1)), lax.optimization_barrier(jnp.sum(target * target, 1)), lax.optimization_barrier(jnp.sum(output * target, 1)))

def reference(student, dino_feat, siglip_feat, dino_weight, siglip_weight, send_index, recv_index):
    groups = N_DP * N_REP
    slot_span = groups * CAP
    token_order = jnp.arange(TOKENS, dtype=jnp.int32)
    owner_group = token_order // TOK_DEV
    lookup_table = jnp.zeros((groups * slot_span,), jnp.int32).at[owner_group * slot_span + send_index].set(token_order)
    matched = lookup_table[recv_index // CAP * slot_span + owner_group * CAP + recv_index % CAP]
    dino_part = E1 // N_TSEC
    siglip_part = E2 // N_TSEC

    def block_step(running, block_index):
        row_start = block_index * TOK_DEV
        student_f = lax.dynamic_slice_in_dim(student, row_start, TOK_DEV, 0).astype(jnp.float32)
        picked_rows = lax.dynamic_slice_in_dim(matched, row_start, TOK_DEV, 0)
        dino_target = dino_feat[picked_rows].astype(jnp.float32)
        siglip_target = siglip_feat[picked_rows].astype(jnp.float32)
        centred = student_f - lax.optimization_barrier(jnp.mean(student_f, 1, keepdims=True))
        inv_dev = lax.rsqrt(lax.optimization_barrier(jnp.mean(centred * centred, 1, keepdims=True)) + norm_eps)
        normed = centred * inv_dev
        normed_bf = normed.astype(jnp.bfloat16)
        dino_out = jnp.dot(normed_bf, dino_weight, preferred_element_type=jnp.float32)
        siglip_out = jnp.dot(normed_bf, siglip_weight, preferred_element_type=jnp.float32)
        dino_delta = head_delta(dino_out, dino_target, row_stats(dino_out, dino_target), float(E1))
        siglip_delta = head_delta(siglip_out, siglip_target, row_stats(siglip_out, siglip_target), float(E2))
        normed_grad = jnp.zeros((TOK_DEV, D), jnp.float32)
        for section in range(N_TSEC):
            dino_cols = slice(section * dino_part, (section + 1) * dino_part)
            siglip_cols = slice(section * siglip_part, (section + 1) * siglip_part)
            partial_value = back_product(dino_delta[:, dino_cols], dino_weight[:, dino_cols])
            partial_value = partial_value + back_product(siglip_delta[:, siglip_cols], siglip_weight[:, siglip_cols])
            rounded = lax.optimization_barrier(partial_value.astype(jnp.bfloat16))
            normed_grad = normed_grad + rounded.astype(jnp.float32)
        grad_mean = lax.optimization_barrier(jnp.mean(normed_grad, 1, keepdims=True))
        grad_proj = lax.optimization_barrier(jnp.mean(normed_grad * normed, 1, keepdims=True))
        feature_grad = ((normed_grad - grad_mean - normed * grad_proj) * inv_dev).astype(jnp.bfloat16)
        dino_sum = running[0] + lax.dot_general(normed_bf, dino_delta, (((0,), (0,)), ((), ())), preferred_element_type=jnp.float32)
        siglip_sum = running[1] + lax.dot_general(normed_bf, siglip_delta, (((0,), (0,)), ((), ())), preferred_element_type=jnp.float32)
        return ((dino_sum, siglip_sum), feature_grad)
    start_sums = (jnp.zeros((D, E1), jnp.float32), jnp.zeros((D, E2), jnp.float32))
    (dino_sum, siglip_sum), row_grads = lax.scan(block_step, start_sums, jnp.arange(groups, dtype=jnp.int32))
    grad_scale = 1.0 / math.sqrt(TOKENS)
    return (row_grads.reshape(TOKENS, D), dino_sum * grad_scale, siglip_sum * grad_scale)
```

```python
import math

import jax
import jax.numpy as jnp
from jax import lax
from jax.experimental import pallas as pl
from jax.experimental.pallas import tpu as pltpu
from jax.sharding import PartitionSpec as P

E1 = 1536
E2 = 1152
CHUNKS = ((0, 32), (32, 32))

norm_eps = 1e-05
length_eps = 1e-06
MESH = pl.DeviceIdType.MESH
BF = jnp.bfloat16
F32 = jnp.float32


def exact_pick(hit, table):
    return jnp.dot(hit.astype(BF), table, preferred_element_type=F32).astype(BF)


def back_product(left_op, right_op):
    return lax.dot_general(
        left_op, right_op, (((1,), (1,)), ((), ())), preferred_element_type=F32
    )


def outer_product(left_op, right_op):
    return lax.dot_general(
        left_op, right_op, (((0,), (0,)), ((), ())), preferred_element_type=F32
    )


def head_delta(outputs, targets, head_width):
    out_sq = sum(jnp.sum(y * y, 1, keepdims=True) for y in outputs)
    tgt_sq = sum(jnp.sum(f * f, 1, keepdims=True) for f in targets)
    cross = sum(jnp.sum(y * f, 1, keepdims=True) for y, f in zip(outputs, targets))
    out_len = jnp.sqrt(out_sq + length_eps)
    tgt_len = jnp.sqrt(tgt_sq + length_eps)
    cosine = cross / (out_len * tgt_len)
    pull_f = head_width / (out_len * tgt_len)
    pull_y = head_width * cosine / (out_len * out_len)
    return [
        (jnp.clip(y - f, -1.0, 1.0) - (pull_f * f - pull_y * y)).astype(BF)
        for y, f in zip(outputs, targets)
    ]


def place():
    dp = lax.axis_index("dp")
    x = lax.axis_index("rep") * 2 + lax.axis_index("tsec")
    return x, dp // 8, (dp // 2) % 4, dp % 2


def at_place(x, y, z, c):
    return {"tsec": x % 2, "dp": (y * 4 + z) * 2 + c, "rep": x // 2}


def sum_kernel(part_ref, out_ref, held, pair, far_y, far_z, far_y2, far_z2, far_x, stage,
               own_sem, pair_send, pair_recv, send_sem, recv_sem):
    x, y, z, c = place()
    t = x % 2
    barrier = pltpu.get_barrier_semaphore()

    def greet(device):
        pl.semaphore_signal(barrier, inc=1, device_id=device, device_id_type=MESH)

    greet(at_place(x, y, z, 1 - c))
    for j in (1, 2, 3):
        greet(at_place(x, (y + j) % 4, z, c))
        greet(at_place(x, y, (z + j) % 4, c))
        greet(at_place((x + j) % 4, y, z, c))
    pl.semaphore_wait(barrier, 10)

    order = (2, 1, 3, 0)

    def pair_copy(k, j, i):
        line = (y + j) % 4 if k == 0 else (z + j) % 4
        src = part_ref.at[0, line, :, 1 - c] if k == 0 else part_ref.at[1, :, line, 1 - c]
        return pltpu.make_async_remote_copy(
            src_ref=src, dst_ref=pair.at[k, j], send_sem=pair_send.at[i], recv_sem=pair_recv.at[i],
            device_id=at_place(x, y, z, 1 - c), device_id_type=MESH)

    def own_copy(k, j, i):
        line = (y + j) % 4 if k == 0 else (z + j) % 4
        src = part_ref.at[0, line, :, c] if k == 0 else part_ref.at[1, :, line, c]
        return pltpu.make_async_copy(src, held.at[k, j], own_sem.at[i])

    def line_copy(k, j, i):
        far = far_y if k == 0 else far_z
        device = at_place(x, (y + j) % 4, z, c) if k == 0 else at_place(x, y, (z + j) % 4, c)
        return pltpu.make_async_remote_copy(
            src_ref=held.at[k, j], dst_ref=far.at[j - 1], send_sem=send_sem.at[i], recv_sem=recv_sem.at[i],
            device_id=device, device_id_type=MESH)

    steps = [(k, j) for j in order for k in (0, 1)]
    for i, (k, j) in enumerate(steps):
        pair_copy(k, j, i).start()
        own_copy(k, j, i).start()
    for i, (k, j) in enumerate(steps):
        own_copy(k, j, i).wait()
        pair_copy(k, j, i).wait_recv()

        @pl.loop(0, 4)
        def _(b, k=k, j=j):
            held[k, j, b] = (held[k, j, b].astype(F32) + pair[k, j, b].astype(F32)).astype(BF)

        if j:
            line_copy(k, j, k * 3 + j - 1).start()
    for i, (k, j) in enumerate(steps):
        pair_copy(k, j, i).wait_send()
    for k in (0, 1):
        for j in (2, 1, 3):
            line_copy(k, j, k * 3 + j - 1).wait()
        far = far_y if k == 0 else far_z

        @pl.loop(0, 4)
        def _(b, k=k, far=far):
            held[k, 0, b] = (held[k, 0, b].astype(F32) + far[0, b].astype(F32)
                             + far[1, b].astype(F32) + far[2, b].astype(F32)).astype(BF)

    def cross_copy(k, j):
        far = far_z2 if k == 0 else far_y2
        b = (z + j) % 4 if k == 0 else (y + j) % 4
        device = at_place(x, y, b, c) if k == 0 else at_place(x, b, z, c)
        i = 6 + k * 3 + j - 1
        return pltpu.make_async_remote_copy(
            src_ref=held.at[k, 0, b], dst_ref=far.at[j - 1], send_sem=send_sem.at[i], recv_sem=recv_sem.at[i],
            device_id=device, device_id_type=MESH)

    for k in (0, 1):
        for j in (2, 1, 3):
            cross_copy(k, j).start()
    for k in (0, 1):
        for j in (2, 1, 3):
            cross_copy(k, j).wait()
        far = far_z2 if k == 0 else far_y2
        mine = held[k, 0, z] if k == 0 else held[k, 0, y]
        stage[k] = (mine.astype(F32) + far[0].astype(F32) + far[1].astype(F32) + far[2].astype(F32)).astype(BF)

    def x_copy(j):
        device = (x + j) % 4
        i = 12 + j - 1
        return pltpu.make_async_remote_copy(
            src_ref=stage.at[device % 2], dst_ref=far_x.at[j - 1], send_sem=send_sem.at[i], recv_sem=recv_sem.at[i],
            device_id=at_place(device, y, z, c), device_id_type=MESH)

    for j in (2, 1, 3):
        x_copy(j).start()
    for j in (2, 1, 3):
        x_copy(j).wait()
    out_ref[...] = (stage[t].astype(F32) + far_x[0].astype(F32) + far_x[1].astype(F32) + far_x[2].astype(F32))


def sum_parts(part):
    rows, width = part.shape[-2:]
    block = (rows, width)
    return pl.pallas_call(
        sum_kernel,
        out_shape=jax.ShapeDtypeStruct(block, F32),
        in_specs=[pl.BlockSpec(memory_space=pl.ANY)],
        out_specs=pl.BlockSpec(memory_space=pltpu.VMEM),
        scratch_shapes=[
            pltpu.VMEM((2, 4, 4) + block, BF),
            pltpu.VMEM((2, 4, 4) + block, BF),
            pltpu.VMEM((3, 4) + block, BF),
            pltpu.VMEM((3, 4) + block, BF),
            pltpu.VMEM((3,) + block, BF),
            pltpu.VMEM((3,) + block, BF),
            pltpu.VMEM((3,) + block, BF),
            pltpu.VMEM((2,) + block, BF),
            pltpu.SemaphoreType.DMA((8,)),
            pltpu.SemaphoreType.DMA((8,)),
            pltpu.SemaphoreType.DMA((8,)),
            pltpu.SemaphoreType.DMA((15,)),
            pltpu.SemaphoreType.DMA((15,)),
        ],
        compiler_params=pltpu.CompilerParams(
            collective_id=0, has_side_effects=True, vmem_limit_bytes=40 * 2**20
        ),
    )(part)


def per_device(student, dino_feat, siglip_feat, dino_weight, siglip_weight, send_index, recv_index):
    groups = lax.axis_size("dp") * lax.axis_size("rep")
    row_count = student.shape[0]
    capacity = 2 * row_count // groups
    dino_cols = dino_feat.shape[1]
    t = lax.axis_index("tsec")
    rep = lax.axis_index("rep")
    first = t == 0
    swap = [(0, 1), (1, 0)]
    n_dp = lax.axis_size("dp")
    mirrored = [
        [((tt ^ r) * n_dp + d) * 2 + r for d in range(n_dp) for r in range(2)] for tt in range(2)
    ]

    teacher = jnp.concatenate([dino_feat, siglip_feat], 1)
    weight_own = jnp.concatenate([dino_weight, siglip_weight], 1)
    weight_far = lax.ppermute(weight_own, "tsec", swap)
    weights = (jnp.where(first, weight_own, weight_far), jnp.where(first, weight_far, weight_own))

    def slot_codes(start, size):
        group = lax.broadcasted_iota(jnp.int32, (groups, size), 0)
        slot = lax.broadcasted_iota(jnp.int32, (groups, size), 1)
        return (group * capacity + slot + start).reshape(-1)

    inboxes = []
    for start, size in CHUNKS:
        codes = slot_codes(start, size)
        outbox = exact_pick(codes[:, None] == send_index[None, :], teacher)
        arrived = lax.all_to_all(
            outbox.reshape(groups, size, -1),
            ("tsec", "dp", "rep"),
            split_axis=0,
            concat_axis=0,
            axis_index_groups=mirrored,
            tiled=True,
        )
        inboxes.append((codes, arrived.reshape(groups * size, -1)))

    key = (recv_index % capacity) * groups + recv_index // capacity
    rank = jnp.sum((key[:, None] > key[None, :]).astype(jnp.int32), 1)
    ranks = jnp.arange(row_count, dtype=jnp.int32)
    code_at = jnp.sum(jnp.where(rank[None, :] == ranks[:, None], recv_index[None, :], 0), 1)

    wgrads = [0.0, 0.0]
    feature_grad = 0.0
    for index, (start, size) in enumerate(CHUNKS):
        begin = row_count * start // capacity
        half = row_count * size // capacity // 2
        mine = begin + t * half
        other = begin + (1 - t) * half
        code_mine = lax.dynamic_slice(code_at, (mine,), (half,))
        code_other = lax.dynamic_slice(code_at, (other,), (half,))

        def aligned(code):
            total = 0
            for codes, rows in inboxes[: index + 1]:
                total = total + exact_pick(code[:, None] == codes[None, :], rows)
            return total

        near = aligned(code_mine)
        far = lax.ppermute(aligned(code_other), "tsec", swap)
        direct = (((code_mine // capacity) % 2 == rep) == first)[:, None]
        halves = [jnp.where(direct, near, far).astype(F32), jnp.where(direct, far, near).astype(F32)]

        pos_mine = mine + jnp.arange(half, dtype=jnp.int32)
        pos_other = other + jnp.arange(half, dtype=jnp.int32)
        student_f = exact_pick(pos_mine[:, None] == rank[None, :], student).astype(F32)
        centred = student_f - jnp.mean(student_f, 1, keepdims=True)
        inv_dev = lax.rsqrt(jnp.mean(centred * centred, 1, keepdims=True) + norm_eps)
        normed = centred * inv_dev
        normed_bf = normed.astype(BF)
        outs = [jnp.dot(normed_bf, w, preferred_element_type=F32) for w in weights]
        dino = head_delta([y[:, :dino_cols] for y in outs], [f[:, :dino_cols] for f in halves], float(E1))
        siglip = head_delta([y[:, dino_cols:] for y in outs], [f[:, dino_cols:] for f in halves], float(E2))
        deltas = [jnp.concatenate([d, s], 1) for d, s in zip(dino, siglip)]
        wgrads = [g + outer_product(normed_bf, d) for g, d in zip(wgrads, deltas)]
        normed_grad = sum(back_product(d, w).astype(BF).astype(F32) for d, w in zip(deltas, weights))
        grad_mean = jnp.mean(normed_grad, 1, keepdims=True)
        grad_proj = jnp.mean(normed_grad * normed, 1, keepdims=True)
        grad = ((normed_grad - grad_mean - normed * grad_proj) * inv_dev).astype(BF)
        grad_far = lax.ppermute(grad, "tsec", swap)
        feature_grad = feature_grad + exact_pick(rank[:, None] == pos_mine[None, :], grad)
        feature_grad = feature_grad + exact_pick(rank[:, None] == pos_other[None, :], grad_far)

    owners = lax.axis_size("dp")
    part = jnp.stack([
        jnp.pad(g.reshape(owners, -1, g.shape[1]), ((0, 0), (0, 8), (0, 0))).astype(BF) for g in wgrads
    ])
    own_rows = student.shape[1] // owners
    part = part.reshape((2, 4, 4, 2) + part.shape[2:])
    grad_scale = 1.0 / math.sqrt(row_count * groups)
    weight_grad = sum_parts(part)[:own_rows] * grad_scale
    return feature_grad, weight_grad[:, :dino_cols], weight_grad[:, dino_cols:]


def solution(mesh):
    placed = (
        P(("dp", "rep"), None),
        P(("dp", "rep"), "tsec"),
        P(("dp", "rep"), "tsec"),
        P(None, "tsec"),
        P(None, "tsec"),
        P(("dp", "rep")),
        P(("dp", "rep")),
    )
    return jax.shard_map(
        per_device,
        mesh=mesh,
        in_specs=placed,
        out_specs=(P(("dp", "rep"), None), P("dp", "tsec"), P("dp", "tsec")),
        check_vma=False,
    )
```

```python
import functools
import math

import jax
import jax.numpy as jnp
from jax import lax
from jax.experimental import pallas as pl
from jax.experimental.pallas import tpu as pltpu
from jax.sharding import PartitionSpec as P

E1 = 1536
E2 = 1152
CHUNKS = ((0, 32), (32, 32))
TILE = 256

norm_eps = 1e-05
length_eps = 1e-06
MESH = pl.DeviceIdType.MESH
BF = jnp.bfloat16
F32 = jnp.float32
I32 = jnp.int32
HERE = pl.BlockSpec(memory_space=pl.ANY)
VMEM = pl.BlockSpec(memory_space=pltpu.VMEM)


def tile_of(rows):
    return next(size for size in (512, 384, 256, 128, 64, 32, 16) if rows % size == 0)


def whole(shape):
    return pl.BlockSpec(shape, lambda i: (0,) * len(shape), pipeline_mode=pl.Buffered(1))


def tiles(rows, width, first=0):
    return pl.BlockSpec((rows, width), lambda i: (first // rows + i, 0))


def local_call(kernel, steps, in_specs, out_specs, out_shape, *operands):
    return pl.pallas_call(
        kernel,
        grid=(steps,),
        in_specs=in_specs,
        out_specs=out_specs,
        out_shape=out_shape,
        compiler_params=pltpu.CompilerParams(vmem_limit_bytes=56 * 2**20),
        cost_estimate=pl.CostEstimate(flops=2**20, bytes_accessed=2**16, transcendentals=0),
    )(*operands)


def hits(column, first, count):
    return (column == first + lax.broadcasted_iota(I32, (column.shape[0], count), 1)).astype(BF)


def back_product(left_op, right_op):
    return lax.dot_general(
        left_op, right_op, (((1,), (1,)), ((), ())), preferred_element_type=F32
    )


def outbox_kernel(place_ref, dino_ref, siglip_ref, after_ref, out_ref):
    rows, count = out_ref.shape[0], dino_ref.shape[0]
    cols = dino_ref.shape[1]
    row = pl.program_id(0) * rows + lax.broadcasted_iota(I32, (rows, count), 0)
    hit = (row == place_ref[...]).astype(BF)
    out_ref[:, :cols] = jnp.dot(hit, dino_ref[...], preferred_element_type=F32).astype(BF)
    out_ref[:, cols:] = back_product(hit, siglip_ref[...]).astype(BF)


def fill_outbox(place, dino_feat, siglip_feat, rows, after):
    width = dino_feat.shape[1] + siglip_feat.shape[0]
    tile = tile_of(rows)
    return local_call(
        outbox_kernel, rows // tile,
        [whole((1, place.shape[1])), whole(dino_feat.shape), whole(siglip_feat.shape), HERE],
        tiles(tile, width), jax.ShapeDtypeStruct((rows, width), BF),
        place, dino_feat, siglip_feat, after)


def greet(devices):
    barrier = pltpu.get_barrier_semaphore()
    for device in devices:
        pl.semaphore_signal(barrier, inc=1, device_id=device, device_id_type=MESH)
    pl.semaphore_wait(barrier, len(devices))


def tile_at(i, start=0):
    return pl.ds(pl.multiple_of(start + i * TILE, TILE), TILE)


def remote(src, dst, send_sem, recv_sem, device):
    return pltpu.make_async_remote_copy(
        src_ref=src, dst_ref=dst, send_sem=send_sem, recv_sem=recv_sem, device_id=device, device_id_type=MESH)


def forward_kernel(columns_ref, rank_ref, place_ref, student_ref, dino_feat_ref, siglip_feat_ref, dino_ref, siglip_ref,
                   after_ref, normed_ref, bf_ref, inv_ref, out_ref, out_far_ref, dino_far_ref, siglip_far_ref,
                   outbox_ref, send_sem, recv_sem):
    dp, t = lax.axis_index("dp"), lax.axis_index("tsec")
    core = dp % 2
    partner, sibling = {"tsec": 1 - t}, {"dp": dp + 1 - 2 * core}
    greet([partner, sibling])
    cols = dino_ref.shape[1]

    fetches, swaps = [], []
    for i, (own, far) in enumerate(((dino_ref, dino_far_ref), (siglip_ref, siglip_far_ref))):
        size = own.shape[0] // 2
        part = pl.ds(pl.multiple_of(core * size, 16), size)
        fetches.append(remote(own.at[part], far.at[part], send_sem.at[i], recv_sem.at[i], partner))
        swaps.append(remote(far.at[part], far.at[part], send_sem.at[2 + i], recv_sem.at[2 + i], sibling))
    for copy in fetches:
        copy.start()

    @pl.loop(0, outbox_ref.shape[0] // TILE)
    def _(i):
        count = dino_feat_ref.shape[0]
        row = i * TILE + lax.broadcasted_iota(I32, (TILE, count), 0)
        hit = (row == place_ref[...]).astype(BF)
        outbox_ref[tile_at(i), :cols] = jnp.dot(hit, dino_feat_ref[...], preferred_element_type=F32).astype(BF)
        outbox_ref[tile_at(i), cols:] = back_product(hit, siglip_feat_ref[...]).astype(BF)

    @pl.loop(0, out_ref.shape[0] // TILE)
    def _(i):
        hit = (columns_ref[tile_at(i), 0:1] == rank_ref[...]).astype(BF)
        rows = jnp.dot(hit, student_ref[...], preferred_element_type=F32)
        centred = rows - jnp.mean(rows, 1, keepdims=True)
        inv_dev = lax.rsqrt(jnp.mean(centred * centred, 1, keepdims=True) + norm_eps)
        normed = centred * inv_dev
        normed_bf = normed.astype(BF)
        normed_ref[tile_at(i)] = normed
        bf_ref[tile_at(i)] = normed_bf
        inv_ref[tile_at(i)] = inv_dev
        out_ref[tile_at(i), :cols] = jnp.dot(normed_bf, dino_ref[...], preferred_element_type=F32)
        out_ref[tile_at(i), cols:] = back_product(normed_bf, siglip_ref[...])

    for copy, swap in zip(fetches, swaps):
        copy.wait_recv()
        swap.start()
    for swap in swaps:
        swap.wait_recv()

    @pl.loop(0, out_ref.shape[0] // TILE)
    def _(i):
        normed_bf = bf_ref[tile_at(i)]
        out_far_ref[tile_at(i), :cols] = jnp.dot(normed_bf, dino_far_ref[...], preferred_element_type=F32)
        out_far_ref[tile_at(i), cols:] = back_product(normed_bf, siglip_far_ref[...])

    for copy in fetches + swaps:
        copy.wait_send()


def forward(columns, rank, place, student, dino_feat, siglip_feat, weights, rows_out, after):
    rows, features = columns.shape[0], student.shape[1]
    width = weights[0].shape[1] + weights[1].shape[0]
    return pl.pallas_call(
        forward_kernel,
        in_specs=[VMEM] * 8 + [HERE],
        out_specs=[VMEM] * 8,
        out_shape=[
            jax.ShapeDtypeStruct((rows, features), F32), jax.ShapeDtypeStruct((rows, features), BF),
            jax.ShapeDtypeStruct((rows, 1), F32), jax.ShapeDtypeStruct((rows, width), F32),
            jax.ShapeDtypeStruct((rows, width), F32), jax.ShapeDtypeStruct(weights[0].shape, BF),
            jax.ShapeDtypeStruct(weights[1].shape, BF), jax.ShapeDtypeStruct((rows_out, width), BF)],
        scratch_shapes=[pltpu.SemaphoreType.DMA((4,)), pltpu.SemaphoreType.DMA((4,))],
        compiler_params=pltpu.CompilerParams(
            collective_id=1, has_side_effects=True, vmem_limit_bytes=60 * 2**20),
        cost_estimate=pl.CostEstimate(flops=3 * 10**10, bytes_accessed=5 * 10**7, transcendentals=0),
    )(columns, rank, place, student, dino_feat, siglip_feat, *weights, after)


def head_delta(outputs, targets, head_width):
    out_sq = sum(jnp.sum(y * y, 1, keepdims=True) for y in outputs)
    tgt_sq = sum(jnp.sum(f * f, 1, keepdims=True) for f in targets)
    cross = sum(jnp.sum(y * f, 1, keepdims=True) for y, f in zip(outputs, targets))
    out_len = jnp.sqrt(out_sq + length_eps)
    tgt_len = jnp.sqrt(tgt_sq + length_eps)
    cosine = cross / (out_len * tgt_len)
    pull_f = head_width / (out_len * tgt_len)
    pull_y = head_width * cosine / (out_len * out_len)
    return [
        (jnp.clip(y - f, -1.0, 1.0) - (pull_f * f - pull_y * y)).astype(BF)
        for y, f in zip(outputs, targets)
    ]


def block_kernel(stage, columns_ref, columns_far_ref, inv_ref, inbox_ref, out_ref, out_far_ref, normed_ref,
                 dino_ref, siglip_ref, dino_far_ref, siglip_far_ref, *refs):
    if stage == 0:
        delta_ref, delta_far_ref, grad_ref, base_far_ref, base_ref = refs[:5]
        refs = refs[5:]
    else:
        base_far_ref, base_ref, _, delta_ref, delta_far_ref, grad_ref = refs[:6]
        refs = refs[6:]
    table, out, out_far, normed_all, dino_w, siglip_w, dino_far_w, siglip_far_w, sent, came, near_all = refs[:11]
    copy_sem, send_sem, recv_sem = refs[11:]
    rows = delta_ref.shape[0]
    first = stage * rows
    cols = dino_w.shape[1]
    loads = [
        pltpu.make_async_copy(src, dst, copy_sem.at[i])
        for i, (src, dst) in enumerate((
            (inbox_ref, table), (dino_ref, dino_w), (siglip_ref, siglip_w), (dino_far_ref, dino_far_w),
            (siglip_far_ref, siglip_far_w), (out_ref.at[pl.ds(first, rows)], out),
            (out_far_ref.at[pl.ds(first, rows)], out_far), (normed_ref.at[pl.ds(first, rows)], normed_all)))
    ]
    for load in loads:
        load.start()
    partner = {"tsec": 1 - lax.axis_index("tsec")}
    greet([partner])

    def swap(i):
        return remote(sent.at[tile_at(i)], came.at[tile_at(i)], send_sem.at[i], recv_sem.at[i], partner)

    def look_up(column):
        hit = (column == lax.broadcasted_iota(I32, (TILE, table.shape[0]), 1)).astype(BF)
        return jnp.dot(hit, table[...], preferred_element_type=F32)

    loads[0].wait()
    steps = rows // TILE
    for i in range(steps):
        found = look_up(columns_far_ref[tile_at(i, first), 2 + stage : 3 + stage])
        if stage:
            found = found + base_far_ref[tile_at(i)].astype(F32)
        sent[tile_at(i)] = found.astype(BF)
        swap(i).start()
    for i in range(steps):
        found = look_up(columns_ref[tile_at(i, first), 2 + stage : 3 + stage])
        if stage:
            found = found + base_ref[tile_at(i)].astype(F32)
        near_all[tile_at(i)] = found.astype(BF)
    if stage == 0:
        for i in range(steps):
            base_far_ref[tile_at(i)] = look_up(columns_far_ref[tile_at(i, rows), 2:3]).astype(BF)
            base_ref[tile_at(i)] = look_up(columns_ref[tile_at(i, rows), 2:3]).astype(BF)
    for load in loads[1:]:
        load.wait()
    for i in range(steps):
        swap(i).wait_recv()
        near, far = near_all[tile_at(i)].astype(F32), came[tile_at(i)].astype(F32)
        direct = columns_ref[tile_at(i, first), 1:2] > 0
        own = jnp.where(direct, near, far)
        other = jnp.where(direct, far, near)
        y, y_far = out[tile_at(i)], out_far[tile_at(i)]
        dino = head_delta([y[:, :cols], y_far[:, :cols]], [own[:, :cols], other[:, :cols]], float(E1))
        siglip = head_delta([y[:, cols:], y_far[:, cols:]], [own[:, cols:], other[:, cols:]], float(E2))
        for delta, d, g in ((delta_ref, dino[0], siglip[0]), (delta_far_ref, dino[1], siglip[1])):
            delta[tile_at(i), :cols] = d
            delta[tile_at(i), cols:] = g
        part = back_product(dino[0], dino_w[...]) + jnp.dot(siglip[0], siglip_w[...], preferred_element_type=F32)
        part_far = back_product(dino[1], dino_far_w[...]) + jnp.dot(
            siglip[1], siglip_far_w[...], preferred_element_type=F32)
        normed_grad = part.astype(BF).astype(F32) + part_far.astype(BF).astype(F32)
        normed = normed_all[tile_at(i)]
        grad_mean = jnp.mean(normed_grad, 1, keepdims=True)
        grad_proj = jnp.mean(normed_grad * normed, 1, keepdims=True)
        inv_dev = inv_ref[tile_at(i, first)]
        grad_ref[tile_at(i)] = ((normed_grad - grad_mean - normed * grad_proj) * inv_dev).astype(BF)
    for i in range(steps):
        swap(i).wait_send()


def handle_block(stage, columns, columns_far, inv_dev, inbox, out, out_far, normed, weights, bases):
    rows, features = normed.shape[0] // 2, normed.shape[1]
    width = inbox.shape[1]
    wide, thin = jax.ShapeDtypeStruct((rows, width), BF), jax.ShapeDtypeStruct((rows, features), BF)
    shapes = [wide, wide, thin] + ([wide, wide] if stage == 0 else [])
    return pl.pallas_call(
        functools.partial(block_kernel, stage),
        in_specs=[VMEM] * 3 + [HERE] * 8 + ([VMEM, VMEM, HERE] if stage else []),
        out_specs=[VMEM] * len(shapes),
        out_shape=shapes,
        scratch_shapes=[
            pltpu.VMEM(inbox.shape, BF), pltpu.VMEM((rows, width), F32), pltpu.VMEM((rows, width), F32),
            pltpu.VMEM((rows, features), F32)] + [pltpu.VMEM(w.shape, BF) for w in weights] + [
            pltpu.VMEM((rows, width), BF), pltpu.VMEM((rows, width), BF), pltpu.VMEM((rows, width), BF),
            pltpu.SemaphoreType.DMA((8,)), pltpu.SemaphoreType.DMA((rows // TILE,)),
            pltpu.SemaphoreType.DMA((rows // TILE,))],
        compiler_params=pltpu.CompilerParams(
            collective_id=2 + stage, has_side_effects=True, vmem_limit_bytes=60 * 2**20),
        cost_estimate=pl.CostEstimate(flops=10**10, bytes_accessed=3 * 10**7, transcendentals=0),
    )(columns, columns_far, inv_dev, inbox, out, out_far, normed, *weights, *bases)


def wgrad_kernel(n, bf_ref, *refs):
    deltas, base, part_ref = refs[:n], refs[n:-1], refs[-1]
    blocks, rows = part_ref.shape[1], bf_ref.shape[1] // part_ref.shape[1]
    for side in (0, 1):
        total, start = 0.0, 0
        for delta in deltas[side::2]:
            size = delta.shape[0]
            total = total + lax.dot_general(
                bf_ref[start : start + size], delta[...], (((0,), (0,)), ((), ())), preferred_element_type=F32)
            start += size
        for b in range(blocks):
            value = total[b * rows : (b + 1) * rows]
            if base:
                value = value + base[0][side, b, :rows].astype(F32)
            part_ref[side, b, :rows] = value.astype(BF)
            part_ref[side, b, rows:] = jnp.zeros((part_ref.shape[2] - rows, part_ref.shape[3]), BF)


def wgrad_part(normed_bf, deltas, first, owners, padded, base=None):
    features = normed_bf.shape[1]
    rows = sum(d.shape[0] for d in deltas[::2])
    width = deltas[0].shape[1]
    split = 2
    blocks = pl.BlockSpec((2, owners // split, padded, width), lambda i: (0, i, 0, 0))
    more = [] if base is None else [base]
    return pl.pallas_call(
        functools.partial(wgrad_kernel, len(deltas)),
        grid=(split,),
        in_specs=[pl.BlockSpec((rows, features // split), lambda i: (first // rows, i))]
        + [whole(d.shape) for d in deltas] + [blocks for _ in more],
        out_specs=blocks,
        out_shape=jax.ShapeDtypeStruct((2, owners, padded, width), BF),
        compiler_params=pltpu.CompilerParams(vmem_limit_bytes=58 * 2**20),
        cost_estimate=pl.CostEstimate(flops=2**20, bytes_accessed=2**16, transcendentals=0),
    )(normed_bf, *deltas, *more)


def unpick_kernel(n, rank_ref, starts_ref, *refs):
    pieces, base, out_ref = refs[:n], refs[n:-1], refs[-1]
    total = base[0][...].astype(F32) if base else 0.0
    for i, piece in enumerate(pieces):
        hit = hits(rank_ref[...], starts_ref[i], piece.shape[0])
        total = total + jnp.dot(hit, piece[...], preferred_element_type=F32)
    out_ref[...] = total.astype(BF)


def unpick(rank, starts, pieces, base=None):
    rows, width = rank.shape[0], pieces[0].shape[1]
    more = [] if base is None else [base]
    tile = tile_of(rows)
    return local_call(
        lambda *refs: unpick_kernel(len(pieces), *refs), rows // tile,
        [tiles(tile, 1), pl.BlockSpec(memory_space=pltpu.SMEM)] + [whole(p.shape) for p in pieces]
        + [tiles(tile, width) for _ in more],
        tiles(tile, width), jax.ShapeDtypeStruct((rows, width), BF),
        rank, starts, *pieces, *more)


def place():
    dp = lax.axis_index("dp")
    x = lax.axis_index("rep") * 2 + lax.axis_index("tsec")
    return x, dp // 8, (dp // 2) % 4, dp % 2


def at_place(x, y, z, c):
    return {"tsec": x % 2, "dp": (y * 4 + z) * 2 + c, "rep": x // 2}


def sum_kernel(part_ref, out_ref, held, pair, far_y, far_z, far_y2, far_z2, far_x, stage,
               own_sem, pair_send, pair_recv, send_sem, recv_sem):
    x, y, z, c = place()
    t = x % 2
    lines = [[at_place(x, (y + j) % 4, z, c), at_place(x, y, (z + j) % 4, c), at_place((x + j) % 4, y, z, c)]
             for j in (1, 2, 3)]
    greet([at_place(x, y, z, 1 - c)] + sum(lines, []))

    order = (2, 1, 3, 0)

    def pair_copy(k, j, i):
        line = (y + j) % 4 if k == 0 else (z + j) % 4
        src = part_ref.at[t, line, :, 1 - c] if k == 0 else part_ref.at[1 - t, :, line, 1 - c]
        return pltpu.make_async_remote_copy(
            src_ref=src, dst_ref=pair.at[k, j], send_sem=pair_send.at[i], recv_sem=pair_recv.at[i],
            device_id=at_place(x, y, z, 1 - c), device_id_type=MESH)

    def own_copy(k, j, i):
        line = (y + j) % 4 if k == 0 else (z + j) % 4
        src = part_ref.at[t, line, :, c] if k == 0 else part_ref.at[1 - t, :, line, c]
        return pltpu.make_async_copy(src, held.at[k, j], own_sem.at[i])

    def line_copy(k, j, i):
        far = far_y if k == 0 else far_z
        device = at_place(x, (y + j) % 4, z, c) if k == 0 else at_place(x, y, (z + j) % 4, c)
        return pltpu.make_async_remote_copy(
            src_ref=held.at[k, j], dst_ref=far.at[j - 1], send_sem=send_sem.at[i], recv_sem=recv_sem.at[i],
            device_id=device, device_id_type=MESH)

    steps = [(k, j) for j in order for k in (0, 1)]
    for i, (k, j) in enumerate(steps):
        pair_copy(k, j, i).start()
        own_copy(k, j, i).start()
    for i, (k, j) in enumerate(steps):
        own_copy(k, j, i).wait()
        pair_copy(k, j, i).wait_recv()

        @pl.loop(0, 4)
        def _(b, k=k, j=j):
            held[k, j, b] = (held[k, j, b].astype(F32) + pair[k, j, b].astype(F32)).astype(BF)

        if j:
            line_copy(k, j, k * 3 + j - 1).start()
    for i, (k, j) in enumerate(steps):
        pair_copy(k, j, i).wait_send()
    for k in (0, 1):
        for j in (2, 1, 3):
            line_copy(k, j, k * 3 + j - 1).wait()
        far = far_y if k == 0 else far_z

        @pl.loop(0, 4)
        def _(b, k=k, far=far):
            held[k, 0, b] = (held[k, 0, b].astype(F32) + far[0, b].astype(F32)
                             + far[1, b].astype(F32) + far[2, b].astype(F32)).astype(BF)

    def cross_copy(k, j):
        far = far_z2 if k == 0 else far_y2
        b = (z + j) % 4 if k == 0 else (y + j) % 4
        device = at_place(x, y, b, c) if k == 0 else at_place(x, b, z, c)
        i = 6 + k * 3 + j - 1
        return pltpu.make_async_remote_copy(
            src_ref=held.at[k, 0, b], dst_ref=far.at[j - 1], send_sem=send_sem.at[i], recv_sem=recv_sem.at[i],
            device_id=device, device_id_type=MESH)

    for k in (0, 1):
        for j in (2, 1, 3):
            cross_copy(k, j).start()
    for k in (0, 1):
        for j in (2, 1, 3):
            cross_copy(k, j).wait()
        far = far_z2 if k == 0 else far_y2
        mine = held[k, 0, z] if k == 0 else held[k, 0, y]
        stage[k] = (mine.astype(F32) + far[0].astype(F32) + far[1].astype(F32) + far[2].astype(F32)).astype(BF)

    def x_copy(j):
        device = (x + j) % 4
        i = 12 + j - 1
        return pltpu.make_async_remote_copy(
            src_ref=stage.at[device % 2], dst_ref=far_x.at[j - 1], send_sem=send_sem.at[i], recv_sem=recv_sem.at[i],
            device_id=at_place(device, y, z, c), device_id_type=MESH)

    for j in (2, 1, 3):
        x_copy(j).start()
    for j in (2, 1, 3):
        x_copy(j).wait()
    out_ref[...] = (stage[t].astype(F32) + far_x[0].astype(F32) + far_x[1].astype(F32) + far_x[2].astype(F32))


def sum_parts(part):
    rows, width = part.shape[-2:]
    block = (rows, width)
    return pl.pallas_call(
        sum_kernel,
        out_shape=jax.ShapeDtypeStruct(block, F32),
        in_specs=[pl.BlockSpec(memory_space=pl.ANY)],
        out_specs=pl.BlockSpec(memory_space=pltpu.VMEM),
        scratch_shapes=[
            pltpu.VMEM((2, 4, 4) + block, BF),
            pltpu.VMEM((2, 4, 4) + block, BF),
            pltpu.VMEM((3, 4) + block, BF),
            pltpu.VMEM((3, 4) + block, BF),
            pltpu.VMEM((3,) + block, BF),
            pltpu.VMEM((3,) + block, BF),
            pltpu.VMEM((3,) + block, BF),
            pltpu.VMEM((2,) + block, BF),
            pltpu.SemaphoreType.DMA((8,)),
            pltpu.SemaphoreType.DMA((8,)),
            pltpu.SemaphoreType.DMA((8,)),
            pltpu.SemaphoreType.DMA((15,)),
            pltpu.SemaphoreType.DMA((15,)),
        ],
        compiler_params=pltpu.CompilerParams(
            collective_id=0, has_side_effects=True, vmem_limit_bytes=58 * 2**20
        ),
    )(part)


def per_device(student, dino_feat, siglip_feat, dino_weight, siglip_weight, send_index, recv_index):
    n_dp = lax.axis_size("dp")
    groups = n_dp * lax.axis_size("rep")
    row_count = student.shape[0]
    capacity = 2 * row_count // groups
    dino_cols = dino_feat.shape[1]
    t = lax.axis_index("tsec")
    rep = lax.axis_index("rep")
    swap = [(0, 1), (1, 0)]
    mirrored = [
        [((tt ^ r) * n_dp + d) * 2 + r for d in range(n_dp) for r in range(2)] for tt in range(2)
    ]

    own_rows = student.shape[1] // n_dp
    padded = -(-own_rows // 16) * 16

    def place_in(chunk, code):
        start, size = CHUNKS[chunk]
        slot = code % capacity - start
        return jnp.where((slot >= 0) & (slot < size), code // capacity * size + slot, -1)

    def exchange(outbox, chunk):
        arrived = lax.all_to_all(
            outbox.reshape(groups, CHUNKS[chunk][1], -1),
            ("tsec", "dp", "rep"),
            split_axis=0,
            concat_axis=0,
            axis_index_groups=mirrored,
            tiled=True,
        )
        return arrived.reshape(outbox.shape)

    outbox = fill_outbox(
        place_in(0, send_index)[None, :], dino_feat, siglip_feat.T, groups * CHUNKS[0][1], send_index)
    inbox = exchange(outbox, 0)

    key = (recv_index % capacity) * groups + recv_index // capacity
    rank = jnp.sum((key[:, None] > key[None, :]).astype(I32), 1)
    ranks = jnp.arange(row_count, dtype=I32)
    code_at = jnp.sum(jnp.where(rank[None, :] == ranks[:, None], recv_index[None, :], 0), 1)
    quarter = row_count // 4

    def columns_of(whose):
        codes, order = [
            jnp.concatenate([
                lax.dynamic_slice(values, ((2 * stage + whose) * quarter,), (quarter,)) for stage in (0, 1)
            ])
            for values in (code_at, ranks)
        ]
        direct = ((codes // capacity) % 2 == rep).astype(I32)
        return jnp.stack([order, direct] + [place_in(c, codes) for c in range(len(CHUNKS))], 1)

    columns, columns_far = columns_of(t), columns_of(1 - t)
    weights = [dino_weight, siglip_weight.T]
    normed, normed_bf, inv_dev, out, out_far, *weights_far, outbox = forward(
        columns, rank[None, :], place_in(1, send_index)[None, :], student, dino_feat, siglip_feat.T, weights,
        groups * CHUNKS[1][1], outbox)
    weights = weights + weights_far
    inboxes = [inbox, exchange(outbox, 1)]

    part, bases, pieces, starts = None, [], [], []
    for stage in (0, 1):
        delta, delta_far, grad, *bases = handle_block(
            stage, columns, columns_far, inv_dev, inboxes[stage], out, out_far, normed, weights, bases)
        pieces += [grad, lax.ppermute(grad, "tsec", swap)]
        starts += [(2 * stage + t) * quarter, (2 * stage + 1 - t) * quarter]
        part = wgrad_part(normed_bf, [delta, delta_far], stage * quarter, n_dp, padded, part)
        bases = bases + [part]

    part = part.reshape((2, 4, 4, 2) + part.shape[2:])
    grad_scale = 1.0 / math.sqrt(row_count * groups)
    weight_grad = sum_parts(part)[:own_rows] * grad_scale
    feature_grad = unpick(rank[:, None], jnp.stack(starts).astype(I32), pieces)
    return feature_grad, weight_grad[:, :dino_cols], weight_grad[:, dino_cols:]


def solution(mesh):
    placed = (
        P(("dp", "rep"), None),
        P(("dp", "rep"), "tsec"),
        P(("dp", "rep"), "tsec"),
        P(None, "tsec"),
        P(None, "tsec"),
        P(("dp", "rep")),
        P(("dp", "rep")),
    )
    return jax.shard_map(
        per_device,
        mesh=mesh,
        in_specs=placed,
        out_specs=(P(("dp", "rep"), None), P("dp", "tsec"), P("dp", "tsec")),
        check_vma=False,
    )
```

```python
import functools
import math

import jax
import jax.numpy as jnp
from jax import lax
from jax.experimental import pallas as pl
from jax.experimental.pallas import tpu as pltpu
from jax.sharding import PartitionSpec as P

E1 = 1536
E2 = 1152
CHUNKS = ((0, 32), (32, 32))
TILE = 256

norm_eps = 1e-05
length_eps = 1e-06
MESH = pl.DeviceIdType.MESH
BF = jnp.bfloat16
F32 = jnp.float32
I32 = jnp.int32
HERE = pl.BlockSpec(memory_space=pl.ANY)
VMEM = pl.BlockSpec(memory_space=pltpu.VMEM)


def tile_of(rows):
    return next(size for size in (512, 384, 256, 128, 64, 32, 16) if rows % size == 0)


def whole(shape):
    return pl.BlockSpec(shape, lambda i: (0,) * len(shape), pipeline_mode=pl.Buffered(1))


def tiles(rows, width, first=0):
    return pl.BlockSpec((rows, width), lambda i: (first // rows + i, 0))


def local_call(kernel, steps, in_specs, out_specs, out_shape, *operands):
    return pl.pallas_call(
        kernel,
        grid=(steps,),
        in_specs=in_specs,
        out_specs=out_specs,
        out_shape=out_shape,
        compiler_params=pltpu.CompilerParams(vmem_limit_bytes=56 * 2**20),
        cost_estimate=pl.CostEstimate(flops=2**20, bytes_accessed=2**16, transcendentals=0),
    )(*operands)


def hits(column, first, count):
    return (column == first + lax.broadcasted_iota(I32, (column.shape[0], count), 1)).astype(BF)


def back_product(left_op, right_op):
    return lax.dot_general(
        left_op, right_op, (((1,), (1,)), ((), ())), preferred_element_type=F32
    )


def outbox_kernel(place_ref, dino_ref, siglip_ref, after_ref, out_ref):
    rows, count = out_ref.shape[0], dino_ref.shape[0]
    cols = dino_ref.shape[1]
    row = pl.program_id(0) * rows + lax.broadcasted_iota(I32, (rows, count), 0)
    hit = (row == place_ref[...]).astype(BF)
    out_ref[:, :cols] = jnp.dot(hit, dino_ref[...], preferred_element_type=F32).astype(BF)
    out_ref[:, cols:] = back_product(hit, siglip_ref[...]).astype(BF)


def fill_outbox(place, dino_feat, siglip_feat, rows, after):
    width = dino_feat.shape[1] + siglip_feat.shape[0]
    tile = tile_of(rows)
    return local_call(
        outbox_kernel, rows // tile,
        [whole((1, place.shape[1])), whole(dino_feat.shape), whole(siglip_feat.shape), HERE],
        tiles(tile, width), jax.ShapeDtypeStruct((rows, width), BF),
        place, dino_feat, siglip_feat, after)


def greet(devices):
    barrier = pltpu.get_barrier_semaphore()
    for device in devices:
        pl.semaphore_signal(barrier, inc=1, device_id=device, device_id_type=MESH)
    pl.semaphore_wait(barrier, len(devices))


def tile_at(i, start=0):
    return pl.ds(pl.multiple_of(start + i * TILE, TILE), TILE)


def remote(src, dst, send_sem, recv_sem, device):
    return pltpu.make_async_remote_copy(
        src_ref=src, dst_ref=dst, send_sem=send_sem, recv_sem=recv_sem, device_id=device, device_id_type=MESH)


def forward_kernel(columns_ref, rank_ref, place_ref, student_ref, dino_feat_ref, siglip_feat_ref, dino_ref, siglip_ref,
                   after_ref, normed_ref, bf_ref, inv_ref, out_ref, out_far_ref, dino_far_ref, siglip_far_ref,
                   outbox_ref, send_sem, recv_sem):
    dp, t = lax.axis_index("dp"), lax.axis_index("tsec")
    core = dp % 2
    partner, sibling = {"tsec": 1 - t}, {"dp": dp + 1 - 2 * core}
    greet([partner, sibling])
    cols = dino_ref.shape[1]

    fetches, swaps = [], []
    for i, (own, far) in enumerate(((dino_ref, dino_far_ref), (siglip_ref, siglip_far_ref))):
        size = own.shape[0] // 2
        part = pl.ds(pl.multiple_of(core * size, 16), size)
        fetches.append(remote(own.at[part], far.at[part], send_sem.at[i], recv_sem.at[i], partner))
        swaps.append(remote(far.at[part], far.at[part], send_sem.at[2 + i], recv_sem.at[2 + i], sibling))
    for copy in fetches:
        copy.start()

    @pl.loop(0, outbox_ref.shape[0] // TILE)
    def _(i):
        count = dino_feat_ref.shape[0]
        row = i * TILE + lax.broadcasted_iota(I32, (TILE, count), 0)
        hit = (row == place_ref[...]).astype(BF)
        outbox_ref[tile_at(i), :cols] = jnp.dot(hit, dino_feat_ref[...], preferred_element_type=F32).astype(BF)
        outbox_ref[tile_at(i), cols:] = back_product(hit, siglip_feat_ref[...]).astype(BF)

    @pl.loop(0, out_ref.shape[0] // TILE)
    def _(i):
        hit = (columns_ref[tile_at(i), 0:1] == rank_ref[...]).astype(BF)
        rows = jnp.dot(hit, student_ref[...], preferred_element_type=F32)
        centred = rows - jnp.mean(rows, 1, keepdims=True)
        inv_dev = lax.rsqrt(jnp.mean(centred * centred, 1, keepdims=True) + norm_eps)
        normed = centred * inv_dev
        normed_bf = normed.astype(BF)
        normed_ref[tile_at(i)] = normed
        bf_ref[tile_at(i)] = normed_bf
        inv_ref[tile_at(i)] = inv_dev
        out_ref[tile_at(i), :cols] = jnp.dot(normed_bf, dino_ref[...], preferred_element_type=F32)
        out_ref[tile_at(i), cols:] = back_product(normed_bf, siglip_ref[...])

    for copy, swap in zip(fetches, swaps):
        copy.wait_recv()
        swap.start()
    for swap in swaps:
        swap.wait_recv()

    @pl.loop(0, out_ref.shape[0] // TILE)
    def _(i):
        normed_bf = bf_ref[tile_at(i)]
        out_far_ref[tile_at(i), :cols] = jnp.dot(normed_bf, dino_far_ref[...], preferred_element_type=F32)
        out_far_ref[tile_at(i), cols:] = back_product(normed_bf, siglip_far_ref[...])

    for copy in fetches + swaps:
        copy.wait_send()


def forward(columns, rank, place, student, dino_feat, siglip_feat, weights, rows_out, after):
    rows, features = columns.shape[0], student.shape[1]
    width = weights[0].shape[1] + weights[1].shape[0]
    return pl.pallas_call(
        forward_kernel,
        in_specs=[VMEM] * 8 + [HERE],
        out_specs=[VMEM] * 8,
        out_shape=[
            jax.ShapeDtypeStruct((rows, features), F32), jax.ShapeDtypeStruct((rows, features), BF),
            jax.ShapeDtypeStruct((rows, 1), F32), jax.ShapeDtypeStruct((rows, width), F32),
            jax.ShapeDtypeStruct((rows, width), F32), jax.ShapeDtypeStruct(weights[0].shape, BF),
            jax.ShapeDtypeStruct(weights[1].shape, BF), jax.ShapeDtypeStruct((rows_out, width), BF)],
        scratch_shapes=[pltpu.SemaphoreType.DMA((4,)), pltpu.SemaphoreType.DMA((4,))],
        compiler_params=pltpu.CompilerParams(
            collective_id=1, has_side_effects=True, vmem_limit_bytes=60 * 2**20),
        cost_estimate=pl.CostEstimate(flops=3 * 10**10, bytes_accessed=5 * 10**7, transcendentals=0),
    )(columns, rank, place, student, dino_feat, siglip_feat, *weights, after)


def head_delta(outputs, targets, head_width):
    out_sq = sum(jnp.sum(y * y, 1, keepdims=True) for y in outputs)
    tgt_sq = sum(jnp.sum(f * f, 1, keepdims=True) for f in targets)
    cross = sum(jnp.sum(y * f, 1, keepdims=True) for y, f in zip(outputs, targets))
    out_len = jnp.sqrt(out_sq + length_eps)
    tgt_len = jnp.sqrt(tgt_sq + length_eps)
    cosine = cross / (out_len * tgt_len)
    pull_f = head_width / (out_len * tgt_len)
    pull_y = head_width * cosine / (out_len * out_len)
    return [
        (jnp.clip(y - f, -1.0, 1.0) - (pull_f * f - pull_y * y)).astype(BF)
        for y, f in zip(outputs, targets)
    ]


def block_kernel(stage, columns_ref, columns_far_ref, inv_ref, inbox_ref, out_ref, out_far_ref, normed_ref,
                 dino_ref, siglip_ref, dino_far_ref, siglip_far_ref, *refs):
    if stage == 0:
        delta_ref, delta_far_ref, grad_ref, base_far_ref, base_ref = refs[:5]
        refs = refs[5:]
    else:
        base_far_ref, base_ref, _, delta_ref, delta_far_ref, grad_ref = refs[:6]
        refs = refs[6:]
    table, out, out_far, normed_all, dino_w, siglip_w, dino_far_w, siglip_far_w, sent, came, near_all = refs[:11]
    copy_sem, send_sem, recv_sem = refs[11:]
    rows = delta_ref.shape[0]
    first = stage * rows
    cols = dino_w.shape[1]
    loads = [
        pltpu.make_async_copy(src, dst, copy_sem.at[i])
        for i, (src, dst) in enumerate((
            (inbox_ref, table), (dino_ref, dino_w), (siglip_ref, siglip_w), (dino_far_ref, dino_far_w),
            (siglip_far_ref, siglip_far_w), (out_ref.at[pl.ds(first, rows)], out),
            (out_far_ref.at[pl.ds(first, rows)], out_far), (normed_ref.at[pl.ds(first, rows)], normed_all)))
    ]
    for load in loads:
        load.start()
    partner = {"tsec": 1 - lax.axis_index("tsec")}
    greet([partner])

    def swap(i):
        return remote(sent.at[tile_at(i)], came.at[tile_at(i)], send_sem.at[i], recv_sem.at[i], partner)

    def look_up(column):
        hit = (column == lax.broadcasted_iota(I32, (TILE, table.shape[0]), 1)).astype(BF)
        return jnp.dot(hit, table[...], preferred_element_type=F32)

    loads[0].wait()
    steps = rows // TILE
    for i in range(steps):
        found = look_up(columns_far_ref[tile_at(i, first), 2 + stage : 3 + stage])
        if stage:
            found = found + base_far_ref[tile_at(i)].astype(F32)
        sent[tile_at(i)] = found.astype(BF)
        swap(i).start()
    for i in range(steps):
        found = look_up(columns_ref[tile_at(i, first), 2 + stage : 3 + stage])
        if stage:
            found = found + base_ref[tile_at(i)].astype(F32)
        near_all[tile_at(i)] = found.astype(BF)
    if stage == 0:
        for i in range(steps):
            base_far_ref[tile_at(i)] = look_up(columns_far_ref[tile_at(i, rows), 2:3]).astype(BF)
            base_ref[tile_at(i)] = look_up(columns_ref[tile_at(i, rows), 2:3]).astype(BF)
    for load in loads[1:]:
        load.wait()
    for i in range(steps):
        swap(i).wait_recv()
        near, far = near_all[tile_at(i)].astype(F32), came[tile_at(i)].astype(F32)
        direct = columns_ref[tile_at(i, first), 1:2] > 0
        own = jnp.where(direct, near, far)
        other = jnp.where(direct, far, near)
        y, y_far = out[tile_at(i)], out_far[tile_at(i)]
        dino = head_delta([y[:, :cols], y_far[:, :cols]], [own[:, :cols], other[:, :cols]], float(E1))
        siglip = head_delta([y[:, cols:], y_far[:, cols:]], [own[:, cols:], other[:, cols:]], float(E2))
        for delta, d, g in ((delta_ref, dino[0], siglip[0]), (delta_far_ref, dino[1], siglip[1])):
            delta[tile_at(i), :cols] = d
            delta[tile_at(i), cols:] = g
        part = back_product(dino[0], dino_w[...]) + jnp.dot(siglip[0], siglip_w[...], preferred_element_type=F32)
        part_far = back_product(dino[1], dino_far_w[...]) + jnp.dot(
            siglip[1], siglip_far_w[...], preferred_element_type=F32)
        normed_grad = part.astype(BF).astype(F32) + part_far.astype(BF).astype(F32)
        normed = normed_all[tile_at(i)]
        grad_mean = jnp.mean(normed_grad, 1, keepdims=True)
        grad_proj = jnp.mean(normed_grad * normed, 1, keepdims=True)
        inv_dev = inv_ref[tile_at(i, first)]
        grad_ref[tile_at(i)] = ((normed_grad - grad_mean - normed * grad_proj) * inv_dev).astype(BF)
    for i in range(steps):
        swap(i).wait_send()


def handle_block(stage, columns, columns_far, inv_dev, inbox, out, out_far, normed, weights, bases):
    rows, features = normed.shape[0] // 2, normed.shape[1]
    width = inbox.shape[1]
    wide, thin = jax.ShapeDtypeStruct((rows, width), BF), jax.ShapeDtypeStruct((rows, features), BF)
    shapes = [wide, wide, thin] + ([wide, wide] if stage == 0 else [])
    return pl.pallas_call(
        functools.partial(block_kernel, stage),
        in_specs=[VMEM] * 3 + [HERE] * 8 + ([VMEM, VMEM, HERE] if stage else []),
        out_specs=[VMEM] * len(shapes),
        out_shape=shapes,
        scratch_shapes=[
            pltpu.VMEM(inbox.shape, BF), pltpu.VMEM((rows, width), F32), pltpu.VMEM((rows, width), F32),
            pltpu.VMEM((rows, features), F32)] + [pltpu.VMEM(w.shape, BF) for w in weights] + [
            pltpu.VMEM((rows, width), BF), pltpu.VMEM((rows, width), BF), pltpu.VMEM((rows, width), BF),
            pltpu.SemaphoreType.DMA((8,)), pltpu.SemaphoreType.DMA((rows // TILE,)),
            pltpu.SemaphoreType.DMA((rows // TILE,))],
        compiler_params=pltpu.CompilerParams(
            collective_id=2 + stage, has_side_effects=True, vmem_limit_bytes=60 * 2**20),
        cost_estimate=pl.CostEstimate(flops=10**10, bytes_accessed=3 * 10**7, transcendentals=0),
    )(columns, columns_far, inv_dev, inbox, out, out_far, normed, *weights, *bases)


def wgrad_kernel(n, bf_ref, *refs):
    deltas, base, part_ref = refs[:n], refs[n:-1], refs[-1]
    blocks, rows = part_ref.shape[1], bf_ref.shape[1] // part_ref.shape[1]
    for side in (0, 1):
        total, start = 0.0, 0
        for delta in deltas[side::2]:
            size = delta.shape[0]
            total = total + lax.dot_general(
                bf_ref[start : start + size], delta[...], (((0,), (0,)), ((), ())), preferred_element_type=F32)
            start += size
        for b in range(blocks):
            value = total[b * rows : (b + 1) * rows]
            if base:
                value = value + base[0][side, b, :rows].astype(F32)
            part_ref[side, b, :rows] = value.astype(BF)
            part_ref[side, b, rows:] = jnp.zeros((part_ref.shape[2] - rows, part_ref.shape[3]), BF)


def wgrad_part(normed_bf, deltas, first, owners, padded, base=None):
    features = normed_bf.shape[1]
    rows = sum(d.shape[0] for d in deltas[::2])
    width = deltas[0].shape[1]
    split = 2
    blocks = pl.BlockSpec((2, owners // split, padded, width), lambda i: (0, i, 0, 0))
    more = [] if base is None else [base]
    return pl.pallas_call(
        functools.partial(wgrad_kernel, len(deltas)),
        grid=(split,),
        in_specs=[pl.BlockSpec((rows, features // split), lambda i: (first // rows, i))]
        + [whole(d.shape) for d in deltas] + [blocks for _ in more],
        out_specs=blocks,
        out_shape=jax.ShapeDtypeStruct((2, owners, padded, width), BF),
        compiler_params=pltpu.CompilerParams(vmem_limit_bytes=58 * 2**20),
        cost_estimate=pl.CostEstimate(flops=2**20, bytes_accessed=2**16, transcendentals=0),
    )(normed_bf, *deltas, *more)


def place():
    dp = lax.axis_index("dp")
    x = lax.axis_index("rep") * 2 + lax.axis_index("tsec")
    return x, dp // 8, (dp // 2) % 4, dp % 2


def at_place(x, y, z, c):
    return {"tsec": x % 2, "dp": (y * 4 + z) * 2 + c, "rep": x // 2}


def tail_kernel(scale, part_ref, turned_ref, delta_ref, delta_far_ref, rank_ref, grad0_ref, grad0_far_ref, grad1_ref,
                feature_ref, dino_ref, siglip_ref,
                work, pair, far_y, far_z, far_y2, far_z2, far_x, stage, grad1_far,
                load_sem, pair_send, pair_recv, send_sem, recv_sem):
    x, y, z, c = place()
    t = x % 2
    sibling, partner = at_place(x, y, z, 1 - c), {"tsec": 1 - t}
    loads = [[pltpu.make_async_copy(part_ref.at[h, l], work.at[h, l], load_sem.at[4 * h + l]) for l in range(4)]
             for h in (0, 1)]
    for h in (0, 1):
        for load in loads[h]:
            load.start()
    lines = [[at_place(x, (y + j) % 4, z, c), at_place(x, y, (z + j) % 4, c), at_place((x + j) % 4, y, z, c)]
             for j in (1, 2, 3)]
    greet([sibling] + sum(lines, []))
    back = remote(grad1_ref, grad1_far, send_sem.at[15], recv_sem.at[15], partner)
    back.start()
    rows = feature_ref.shape[1] // 32

    def add_products(h, line):
        delta = delta_ref if h == 0 else delta_far_ref
        features = pl.ds(pl.multiple_of(line * 8 * rows, 16), 8 * rows)
        new = jnp.dot(turned_ref[features], delta[...], preferred_element_type=F32)
        for b in range(8):
            old = work[h, line, b // 2, b % 2, :rows].astype(F32)
            work[h, line, b // 2, b % 2, :rows] = (old + new[b * rows : (b + 1) * rows]).astype(BF)

    def pair_copy(h, j):
        src = work.at[0, (y + j) % 4, :, 1 - c] if h == 0 else work.at[1, :, (z + j) % 4, 1 - c]
        return remote(src, pair.at[h, j], pair_send.at[4 * h + j], pair_recv.at[4 * h + j], sibling)

    order = (2, 1, 3, 0)
    for load in loads[0]:
        load.wait()
    for j in order:
        add_products(0, (y + j) % 4)
        pair_copy(0, j).start()
    for load in loads[1]:
        load.wait()

    @pl.loop(0, 4)
    def _(line):
        add_products(1, line)

    for j in order:
        pair_copy(1, j).start()

    def line_copy(h, j):
        far = far_y if h == 0 else far_z
        device = at_place(x, (y + j) % 4, z, c) if h == 0 else at_place(x, y, (z + j) % 4, c)
        i = 3 * h + j - 1
        return remote(pair.at[h, j], far.at[j - 1], send_sem.at[i], recv_sem.at[i], device)

    for j in order:
        for h in (0, 1):
            pair_copy(h, j).wait_recv()

            @pl.loop(0, 4)
            def _(b, h=h, j=j):
                own = work[0, (y + j) % 4, b, c] if h == 0 else work[1, b, (z + j) % 4, c]
                pair[h, j, b] = (own.astype(F32) + pair[h, j, b].astype(F32)).astype(BF)

            if j:
                line_copy(h, j).start()

    count = grad0_ref.shape[0]
    starts = [(2 * s + side) * count for s in (0, 1) for side in (t, 1 - t)]

    @pl.loop(0, feature_ref.shape[0] // TILE)
    def _(i):
        total = 0.0
        for start, piece in zip(starts, (grad0_ref, grad0_far_ref, grad1_ref)):
            hit = hits(rank_ref[tile_at(i)], start, count)
            total = total + jnp.dot(hit, piece[...], preferred_element_type=F32)
        feature_ref[tile_at(i)] = total.astype(BF)

    for h in (0, 1):
        for j in order:
            pair_copy(h, j).wait_send()

    def cross_copy(h, j):
        far = far_z2 if h == 0 else far_y2
        b = (z + j) % 4 if h == 0 else (y + j) % 4
        device = at_place(x, y, b, c) if h == 0 else at_place(x, b, z, c)
        i = 6 + 3 * h + j - 1
        return remote(pair.at[h, 0, b], far.at[j - 1], send_sem.at[i], recv_sem.at[i], device)

    for h in (0, 1):
        far = far_y if h == 0 else far_z
        for j in (2, 1, 3):
            line_copy(h, j).wait()

        @pl.loop(0, 4)
        def _(b, h=h, far=far):
            pair[h, 0, b] = (pair[h, 0, b].astype(F32) + far[0, b].astype(F32)
                             + far[1, b].astype(F32) + far[2, b].astype(F32)).astype(BF)

        for j in (2, 1, 3):
            cross_copy(h, j).start()

    back.wait()

    @pl.loop(0, feature_ref.shape[0] // TILE)
    def _(i):
        hit = hits(rank_ref[tile_at(i)], starts[3], count)
        found = jnp.dot(hit, grad1_far[...], preferred_element_type=F32)
        feature_ref[tile_at(i)] = (feature_ref[tile_at(i)].astype(F32) + found).astype(BF)

    for h in (0, 1):
        far = far_z2 if h == 0 else far_y2
        for j in (2, 1, 3):
            cross_copy(h, j).wait()
        mine = pair[h, 0, z] if h == 0 else pair[h, 0, y]
        stage[h] = (mine.astype(F32) + far[0].astype(F32) + far[1].astype(F32) + far[2].astype(F32)).astype(BF)

    def x_copy(j):
        device = (x + j) % 4
        i = 12 + j - 1
        return remote(stage.at[(device + x) % 2], far_x.at[j - 1], send_sem.at[i], recv_sem.at[i],
                      at_place(device, y, z, c))

    for j in (2, 1, 3):
        x_copy(j).start()
    for j in (2, 1, 3):
        x_copy(j).wait()
    total = (stage[0].astype(F32) + far_x[0].astype(F32) + far_x[1].astype(F32) + far_x[2].astype(F32)) * scale
    dino_ref[...] = total[:rows, : dino_ref.shape[1]]
    siglip_ref[...] = total[:rows, dino_ref.shape[1] :]


def finish(scale, part, turned, delta, delta_far, rank, grads, dino_cols):
    block = part.shape[-2:]
    count, features = grads[0].shape
    own_rows = features // 32
    return pl.pallas_call(
        functools.partial(tail_kernel, scale),
        out_shape=[
            jax.ShapeDtypeStruct((rank.shape[0], features), BF),
            jax.ShapeDtypeStruct((own_rows, dino_cols), F32),
            jax.ShapeDtypeStruct((own_rows, block[1] - dino_cols), F32)],
        in_specs=[HERE] + [VMEM] * 7,
        out_specs=[VMEM] * 3,
        scratch_shapes=[
            pltpu.VMEM((2, 4, 4, 2) + block, BF),
            pltpu.VMEM((2, 4, 4) + block, BF),
            pltpu.VMEM((3, 4) + block, BF),
            pltpu.VMEM((3, 4) + block, BF),
            pltpu.VMEM((3,) + block, BF),
            pltpu.VMEM((3,) + block, BF),
            pltpu.VMEM((3,) + block, BF),
            pltpu.VMEM((2,) + block, BF),
            pltpu.VMEM((count, features), BF),
            pltpu.SemaphoreType.DMA((8,)),
            pltpu.SemaphoreType.DMA((8,)),
            pltpu.SemaphoreType.DMA((8,)),
            pltpu.SemaphoreType.DMA((16,)),
            pltpu.SemaphoreType.DMA((16,)),
        ],
        compiler_params=pltpu.CompilerParams(
            collective_id=0, has_side_effects=True, vmem_limit_bytes=60 * 2**20
        ),
        cost_estimate=pl.CostEstimate(flops=10**10, bytes_accessed=5 * 10**7, transcendentals=0),
    )(part, turned, delta, delta_far, rank, *grads)


def per_device(student, dino_feat, siglip_feat, dino_weight, siglip_weight, send_index, recv_index):
    n_dp = lax.axis_size("dp")
    groups = n_dp * lax.axis_size("rep")
    row_count = student.shape[0]
    capacity = 2 * row_count // groups
    dino_cols = dino_feat.shape[1]
    t = lax.axis_index("tsec")
    rep = lax.axis_index("rep")
    swap = [(0, 1), (1, 0)]
    mirrored = [
        [((tt ^ r) * n_dp + d) * 2 + r for d in range(n_dp) for r in range(2)] for tt in range(2)
    ]

    own_rows = student.shape[1] // n_dp
    padded = -(-own_rows // 16) * 16

    def place_in(chunk, code):
        start, size = CHUNKS[chunk]
        slot = code % capacity - start
        return jnp.where((slot >= 0) & (slot < size), code // capacity * size + slot, -1)

    def exchange(outbox, chunk):
        arrived = lax.all_to_all(
            outbox.reshape(groups, CHUNKS[chunk][1], -1),
            ("tsec", "dp", "rep"),
            split_axis=0,
            concat_axis=0,
            axis_index_groups=mirrored,
            tiled=True,
        )
        return arrived.reshape(outbox.shape)

    outbox = fill_outbox(
        place_in(0, send_index)[None, :], dino_feat, siglip_feat.T, groups * CHUNKS[0][1], send_index)
    inbox = exchange(outbox, 0)

    key = (recv_index % capacity) * groups + recv_index // capacity
    rank = jnp.sum((key[:, None] > key[None, :]).astype(I32), 1)
    ranks = jnp.arange(row_count, dtype=I32)
    code_at = jnp.sum(jnp.where(rank[None, :] == ranks[:, None], recv_index[None, :], 0), 1)
    quarter = row_count // 4

    def columns_of(whose):
        codes, order = [
            jnp.concatenate([
                lax.dynamic_slice(values, ((2 * stage + whose) * quarter,), (quarter,)) for stage in (0, 1)
            ])
            for values in (code_at, ranks)
        ]
        direct = ((codes // capacity) % 2 == rep).astype(I32)
        return jnp.stack([order, direct] + [place_in(c, codes) for c in range(len(CHUNKS))], 1)

    columns, columns_far = columns_of(t), columns_of(1 - t)
    weights = [dino_weight, siglip_weight.T]
    normed, normed_bf, inv_dev, out, out_far, *weights_far, outbox = forward(
        columns, rank[None, :], place_in(1, send_index)[None, :], student, dino_feat, siglip_feat.T, weights,
        groups * CHUNKS[1][1], outbox)
    weights = weights + weights_far
    inboxes = [inbox, exchange(outbox, 1)]

    turned = normed_bf[quarter:].T
    bases, grads = [], []
    for stage in (0, 1):
        delta, delta_far, grad, *bases = handle_block(
            stage, columns, columns_far, inv_dev, inboxes[stage], out, out_far, normed, weights, bases)
        grads.append(grad)
        if stage == 0:
            grads.append(lax.ppermute(grad, "tsec", swap))
            part = wgrad_part(normed_bf, [delta, delta_far], 0, n_dp, padded)
            bases = bases + [part]

    part = part.reshape((2, 4, 4, 2) + part.shape[2:])
    grad_scale = 1.0 / math.sqrt(row_count * groups)
    return tuple(finish(grad_scale, part, turned, delta, delta_far, rank[:, None], grads, dino_cols))


def solution(mesh):
    placed = (
        P(("dp", "rep"), None),
        P(("dp", "rep"), "tsec"),
        P(("dp", "rep"), "tsec"),
        P(None, "tsec"),
        P(None, "tsec"),
        P(("dp", "rep")),
        P(("dp", "rep")),
    )
    return jax.shard_map(
        per_device,
        mesh=mesh,
        in_specs=placed,
        out_specs=(P(("dp", "rep"), None), P("dp", "tsec"), P("dp", "tsec")),
        check_vma=False,
    )
```

```python
import functools
import math

import jax
import jax.numpy as jnp
from jax import lax
from jax.experimental import pallas as pl
from jax.experimental.pallas import tpu as pltpu
from jax.sharding import PartitionSpec as P

E1 = 1536
E2 = 1152
CHUNKS = ((0, 32), (32, 32))
TILE = 256

norm_eps = 1e-05
length_eps = 1e-06
MESH = pl.DeviceIdType.MESH
BF = jnp.bfloat16
F32 = jnp.float32
I32 = jnp.int32
HERE = pl.BlockSpec(memory_space=pl.ANY)
VMEM = pl.BlockSpec(memory_space=pltpu.VMEM)


def tile_of(rows):
    return next(size for size in (512, 384, 256, 128, 64, 32, 16) if rows % size == 0)


def whole(shape):
    return pl.BlockSpec(shape, lambda i: (0,) * len(shape), pipeline_mode=pl.Buffered(1))


def tiles(rows, width, first=0):
    return pl.BlockSpec((rows, width), lambda i: (first // rows + i, 0))


def local_call(kernel, steps, in_specs, out_specs, out_shape, *operands):
    return pl.pallas_call(
        kernel,
        grid=(steps,),
        in_specs=in_specs,
        out_specs=out_specs,
        out_shape=out_shape,
        compiler_params=pltpu.CompilerParams(vmem_limit_bytes=56 * 2**20),
        cost_estimate=pl.CostEstimate(flops=2**20, bytes_accessed=2**16, transcendentals=0),
    )(*operands)


def hits(column, first, count):
    return (column == first + lax.broadcasted_iota(I32, (column.shape[0], count), 1)).astype(BF)


def back_product(left_op, right_op):
    return lax.dot_general(
        left_op, right_op, (((1,), (1,)), ((), ())), preferred_element_type=F32
    )


def outbox_kernel(place_ref, dino_ref, siglip_ref, after_ref, out_ref):
    rows, count = out_ref.shape[0], dino_ref.shape[0]
    cols = dino_ref.shape[1]
    row = pl.program_id(0) * rows + lax.broadcasted_iota(I32, (rows, count), 0)
    hit = (row == place_ref[...]).astype(BF)
    out_ref[:, :cols] = jnp.dot(hit, dino_ref[...], preferred_element_type=F32).astype(BF)
    out_ref[:, cols:] = back_product(hit, siglip_ref[...]).astype(BF)


def fill_outbox(place, dino_feat, siglip_feat, rows, after):
    width = dino_feat.shape[1] + siglip_feat.shape[0]
    tile = tile_of(rows)
    return local_call(
        outbox_kernel, rows // tile,
        [whole((1, place.shape[1])), whole(dino_feat.shape), whole(siglip_feat.shape), HERE],
        tiles(tile, width), jax.ShapeDtypeStruct((rows, width), BF),
        place, dino_feat, siglip_feat, after)


def greet(devices):
    barrier = pltpu.get_barrier_semaphore()
    for device in devices:
        pl.semaphore_signal(barrier, inc=1, device_id=device, device_id_type=MESH)
    pl.semaphore_wait(barrier, len(devices))


def tile_at(i, start=0, tile=TILE):
    return pl.ds(pl.multiple_of(start + i * tile, tile), tile)


def remote(src, dst, send_sem, recv_sem, device):
    return pltpu.make_async_remote_copy(
        src_ref=src, dst_ref=dst, send_sem=send_sem, recv_sem=recv_sem, device_id=device, device_id_type=MESH)


def forward_kernel(columns_ref, rank_ref, place_ref, student_ref, dino_feat_ref, siglip_feat_ref, dino_ref, siglip_ref,
                   after_ref, normed_ref, bf_ref, inv_ref, out_ref, out_far_ref, dino_far_ref, siglip_far_ref,
                   outbox_ref, send_sem, recv_sem):
    dp, t = lax.axis_index("dp"), lax.axis_index("tsec")
    core = dp % 2
    partner, sibling = {"tsec": 1 - t}, {"dp": dp + 1 - 2 * core}
    greet([partner, sibling])
    cols = dino_ref.shape[1]

    fetches, swaps = [], []
    for i, (own, far) in enumerate(((dino_ref, dino_far_ref), (siglip_ref, siglip_far_ref))):
        size = own.shape[0] // 2
        part = pl.ds(pl.multiple_of(core * size, 16), size)
        fetches.append(remote(own.at[part], far.at[part], send_sem.at[i], recv_sem.at[i], partner))
        swaps.append(remote(far.at[part], far.at[part], send_sem.at[2 + i], recv_sem.at[2 + i], sibling))
    for copy in fetches:
        copy.start()

    @pl.loop(0, outbox_ref.shape[0] // TILE)
    def _(i):
        count = dino_feat_ref.shape[0]
        row = i * TILE + lax.broadcasted_iota(I32, (TILE, count), 0)
        hit = (row == place_ref[...]).astype(BF)
        outbox_ref[tile_at(i), :cols] = jnp.dot(hit, dino_feat_ref[...], preferred_element_type=F32).astype(BF)
        outbox_ref[tile_at(i), cols:] = back_product(hit, siglip_feat_ref[...]).astype(BF)

    @pl.loop(0, out_ref.shape[0] // TILE)
    def _(i):
        hit = (columns_ref[tile_at(i), 0:1] == rank_ref[...]).astype(BF)
        rows = jnp.dot(hit, student_ref[...], preferred_element_type=F32)
        centred = rows - jnp.mean(rows, 1, keepdims=True)
        inv_dev = lax.rsqrt(jnp.mean(centred * centred, 1, keepdims=True) + norm_eps)
        normed = centred * inv_dev
        normed_bf = normed.astype(BF)
        normed_ref[tile_at(i)] = normed
        bf_ref[tile_at(i)] = normed_bf
        inv_ref[tile_at(i)] = inv_dev
        out_ref[tile_at(i), :cols] = jnp.dot(normed_bf, dino_ref[...], preferred_element_type=F32)
        out_ref[tile_at(i), cols:] = back_product(normed_bf, siglip_ref[...])

    for copy, swap in zip(fetches, swaps):
        copy.wait_recv()
        swap.start()
    for swap in swaps:
        swap.wait_recv()

    @pl.loop(0, out_ref.shape[0] // TILE)
    def _(i):
        normed_bf = bf_ref[tile_at(i)]
        out_far_ref[tile_at(i), :cols] = jnp.dot(normed_bf, dino_far_ref[...], preferred_element_type=F32)
        out_far_ref[tile_at(i), cols:] = back_product(normed_bf, siglip_far_ref[...])

    for copy in fetches + swaps:
        copy.wait_send()


def forward(columns, rank, place, student, dino_feat, siglip_feat, weights, rows_out, after):
    rows, features = columns.shape[0], student.shape[1]
    width = weights[0].shape[1] + weights[1].shape[0]
    return pl.pallas_call(
        forward_kernel,
        in_specs=[VMEM] * 8 + [HERE],
        out_specs=[VMEM] * 8,
        out_shape=[
            jax.ShapeDtypeStruct((rows, features), F32), jax.ShapeDtypeStruct((rows, features), BF),
            jax.ShapeDtypeStruct((rows, 1), F32), jax.ShapeDtypeStruct((rows, width), F32),
            jax.ShapeDtypeStruct((rows, width), F32), jax.ShapeDtypeStruct(weights[0].shape, BF),
            jax.ShapeDtypeStruct(weights[1].shape, BF), jax.ShapeDtypeStruct((rows_out, width), BF)],
        scratch_shapes=[pltpu.SemaphoreType.DMA((4,)), pltpu.SemaphoreType.DMA((4,))],
        compiler_params=pltpu.CompilerParams(
            collective_id=1, has_side_effects=True, vmem_limit_bytes=60 * 2**20),
        cost_estimate=pl.CostEstimate(flops=3 * 10**10, bytes_accessed=5 * 10**7, transcendentals=0),
    )(columns, rank, place, student, dino_feat, siglip_feat, *weights, after)


def head_delta(outputs, targets, head_width):
    out_sq = sum(jnp.sum(y * y, 1, keepdims=True) for y in outputs)
    tgt_sq = sum(jnp.sum(f * f, 1, keepdims=True) for f in targets)
    cross = sum(jnp.sum(y * f, 1, keepdims=True) for y, f in zip(outputs, targets))
    out_len = jnp.sqrt(out_sq + length_eps)
    tgt_len = jnp.sqrt(tgt_sq + length_eps)
    cosine = cross / (out_len * tgt_len)
    pull_f = head_width / (out_len * tgt_len)
    pull_y = head_width * cosine / (out_len * out_len)
    return [
        (jnp.clip(y - f, -1.0, 1.0) - (pull_f * f - pull_y * y)).astype(BF)
        for y, f in zip(outputs, targets)
    ]


def block_kernel(stage, columns_ref, columns_far_ref, inv_ref, inbox_ref, out_ref, out_far_ref, normed_ref,
                 dino_ref, siglip_ref, dino_far_ref, siglip_far_ref, *refs):
    if stage == 0:
        delta_ref, delta_far_ref, grad_ref, base_far_ref, base_ref = refs[:5]
        refs = refs[5:]
    else:
        base_far_in, base_in, _, delta_ref, delta_far_ref, grad_ref = refs[:6]
        base_far_ref, base_ref = refs[-2:]
        refs = refs[6:-2]
    table, out, out_far, normed_all, dino_w, siglip_w, dino_far_w, siglip_far_w, sent, came, near_all = refs[:11]
    copy_sem, send_sem, recv_sem = refs[11:]
    rows = delta_ref.shape[0]
    first = stage * rows
    cols = dino_w.shape[1]
    tile = TILE // (1 + stage)
    at = functools.partial(tile_at, tile=tile)
    bases = ((base_far_in, base_far_ref), (base_in, base_ref)) if stage else ()
    loads = [
        pltpu.make_async_copy(src, dst, copy_sem.at[i])
        for i, (src, dst) in enumerate(((inbox_ref, table),) + bases + (
            (dino_ref, dino_w), (siglip_ref, siglip_w), (dino_far_ref, dino_far_w),
            (siglip_far_ref, siglip_far_w), (out_ref.at[pl.ds(first, rows)], out),
            (out_far_ref.at[pl.ds(first, rows)], out_far), (normed_ref.at[pl.ds(first, rows)], normed_all)))
    ]
    for load in loads:
        load.start()
    partner = {"tsec": 1 - lax.axis_index("tsec")}
    greet([partner])

    def swap(i):
        return remote(sent.at[at(i)], came.at[at(i)], send_sem.at[i], recv_sem.at[i], partner)

    def look_up(column):
        hit = (column == lax.broadcasted_iota(I32, (tile, table.shape[0]), 1)).astype(BF)
        return jnp.dot(hit, table[...], preferred_element_type=F32)

    for load in loads[: 1 + len(bases)]:
        load.wait()
    steps = rows // tile
    for i in range(steps):
        found = look_up(columns_far_ref[at(i, first), 2 + stage : 3 + stage])
        if stage:
            found = found + base_far_ref[at(i)].astype(F32)
        sent[at(i)] = found.astype(BF)
        swap(i).start()
    for i in range(steps):
        found = look_up(columns_ref[at(i, first), 2 + stage : 3 + stage])
        if stage:
            found = found + base_ref[at(i)].astype(F32)
        near_all[at(i)] = found.astype(BF)
    if stage == 0:
        for i in range(steps):
            base_far_ref[at(i)] = look_up(columns_far_ref[at(i, rows), 2:3]).astype(BF)
            base_ref[at(i)] = look_up(columns_ref[at(i, rows), 2:3]).astype(BF)
    for load in loads[1 + len(bases) :]:
        load.wait()
    for i in range(steps):
        swap(i).wait_recv()
        near, far = near_all[at(i)].astype(F32), came[at(i)].astype(F32)
        direct = columns_ref[at(i, first), 1:2] > 0
        own = jnp.where(direct, near, far)
        other = jnp.where(direct, far, near)
        y, y_far = out[at(i)], out_far[at(i)]
        dino = head_delta([y[:, :cols], y_far[:, :cols]], [own[:, :cols], other[:, :cols]], float(E1))
        siglip = head_delta([y[:, cols:], y_far[:, cols:]], [own[:, cols:], other[:, cols:]], float(E2))
        for delta, d, g in ((delta_ref, dino[0], siglip[0]), (delta_far_ref, dino[1], siglip[1])):
            delta[at(i), :cols] = d
            delta[at(i), cols:] = g
        part = back_product(dino[0], dino_w[...]) + jnp.dot(siglip[0], siglip_w[...], preferred_element_type=F32)
        part_far = back_product(dino[1], dino_far_w[...]) + jnp.dot(
            siglip[1], siglip_far_w[...], preferred_element_type=F32)
        normed_grad = part.astype(BF).astype(F32) + part_far.astype(BF).astype(F32)
        normed = normed_all[at(i)]
        grad_mean = jnp.mean(normed_grad, 1, keepdims=True)
        grad_proj = jnp.mean(normed_grad * normed, 1, keepdims=True)
        inv_dev = inv_ref[at(i, first)]
        grad_ref[at(i)] = ((normed_grad - grad_mean - normed * grad_proj) * inv_dev).astype(BF)
    for i in range(steps):
        swap(i).wait_send()


def handle_block(stage, columns, columns_far, inv_dev, inbox, out, out_far, normed, weights, bases):
    rows, features = normed.shape[0] // 2, normed.shape[1]
    width = inbox.shape[1]
    wide, thin = jax.ShapeDtypeStruct((rows, width), BF), jax.ShapeDtypeStruct((rows, features), BF)
    shapes = [wide, wide, thin] + ([wide, wide] if stage == 0 else [])
    steps = rows // TILE * (1 + stage)
    return pl.pallas_call(
        functools.partial(block_kernel, stage),
        in_specs=[VMEM] * 3 + [HERE] * (11 if stage else 8),
        out_specs=[VMEM] * len(shapes),
        out_shape=shapes,
        scratch_shapes=[
            pltpu.VMEM(inbox.shape, BF), pltpu.VMEM((rows, width), F32), pltpu.VMEM((rows, width), F32),
            pltpu.VMEM((rows, features), F32)] + [pltpu.VMEM(w.shape, BF) for w in weights] + [
            pltpu.VMEM((rows, width), BF), pltpu.VMEM((rows, width), BF), pltpu.VMEM((rows, width), BF),
            pltpu.SemaphoreType.DMA((10,)), pltpu.SemaphoreType.DMA((steps,)), pltpu.SemaphoreType.DMA((steps,))]
        + [pltpu.VMEM((rows, width), BF) for _ in range(2 * stage)],
        compiler_params=pltpu.CompilerParams(
            collective_id=2 + stage, has_side_effects=True, vmem_limit_bytes=60 * 2**20),
        cost_estimate=pl.CostEstimate(flops=10**10, bytes_accessed=3 * 10**7, transcendentals=0),
    )(columns, columns_far, inv_dev, inbox, out, out_far, normed, *weights, *bases)


def wgrad_kernel(n, bf_ref, *refs):
    deltas, base, part_ref = refs[:n], refs[n:-1], refs[-1]
    blocks, rows = part_ref.shape[1], bf_ref.shape[1] // part_ref.shape[1]
    for side in (0, 1):
        total, start = 0.0, 0
        for delta in deltas[side::2]:
            size = delta.shape[0]
            total = total + lax.dot_general(
                bf_ref[start : start + size], delta[...], (((0,), (0,)), ((), ())), preferred_element_type=F32)
            start += size
        for b in range(blocks):
            value = total[b * rows : (b + 1) * rows]
            if base:
                value = value + base[0][side, b, :rows].astype(F32)
            part_ref[side, b, :rows] = value.astype(BF)
            part_ref[side, b, rows:] = jnp.zeros((part_ref.shape[2] - rows, part_ref.shape[3]), BF)


def wgrad_part(normed_bf, deltas, first, owners, padded, base=None):
    features = normed_bf.shape[1]
    rows = sum(d.shape[0] for d in deltas[::2])
    width = deltas[0].shape[1]
    split = 2
    blocks = pl.BlockSpec((2, owners // split, padded, width), lambda i: (0, i, 0, 0))
    more = [] if base is None else [base]
    return pl.pallas_call(
        functools.partial(wgrad_kernel, len(deltas)),
        grid=(split,),
        in_specs=[pl.BlockSpec((rows, features // split), lambda i: (first // rows, i))]
        + [whole(d.shape) for d in deltas] + [blocks for _ in more],
        out_specs=blocks,
        out_shape=jax.ShapeDtypeStruct((2, owners, padded, width), BF),
        compiler_params=pltpu.CompilerParams(vmem_limit_bytes=58 * 2**20),
        cost_estimate=pl.CostEstimate(flops=2**20, bytes_accessed=2**16, transcendentals=0),
    )(normed_bf, *deltas, *more)


def place():
    dp = lax.axis_index("dp")
    x = lax.axis_index("rep") * 2 + lax.axis_index("tsec")
    return x, dp // 8, (dp // 2) % 4, dp % 2


def at_place(x, y, z, c):
    return {"tsec": x % 2, "dp": (y * 4 + z) * 2 + c, "rep": x // 2}


def tail_kernel(scale, part_ref, turned_ref, delta_ref, delta_far_ref, rank_ref, grad0_ref, grad0_far_ref, grad1_ref,
                feature_ref, dino_ref, siglip_ref,
                work, pair, far_y, far_z, far_y2, far_z2, far_x, stage, grad1_far,
                load_sem, pair_send, pair_recv, send_sem, recv_sem):
    x, y, z, c = place()
    t = x % 2
    sibling, partner = at_place(x, y, z, 1 - c), {"tsec": 1 - t}
    steps = [(h, j) for j in (2, 1, 3, 0) for h in (0, 1)]

    def line_of(h, j):
        return (y + j) % 4 if h == 0 else (z + j) % 4

    def load(h, j):
        line = line_of(h, j)
        src, dst = (r.at[0, line] if h == 0 else r.at[1, :, line] for r in (part_ref, work))
        return pltpu.make_async_copy(src, dst, load_sem.at[4 * h + j])

    for h, j in steps:
        load(h, j).start()
    lines = [[at_place(x, (y + j) % 4, z, c), at_place(x, y, (z + j) % 4, c), at_place((x + j) % 4, y, z, c)]
             for j in (1, 2, 3)]
    greet([sibling] + sum(lines, []))
    back = remote(grad1_ref, grad1_far, send_sem.at[15], recv_sem.at[15], partner)
    back.start()
    rows = feature_ref.shape[1] // 32

    def add_products(h, j):
        delta = delta_ref if h == 0 else delta_far_ref
        line = line_of(h, j)
        features = pl.ds(pl.multiple_of(line * 8 * rows, 16), 8 * rows)
        new = jnp.dot(turned_ref[h, features], delta[...], preferred_element_type=F32)
        for b in range(8):
            at = (0, line, b // 2, b % 2) if h == 0 else (1, b // 2, line, b % 2)
            old = work[at + (slice(0, rows),)].astype(F32)
            work[at + (slice(0, rows),)] = (old + new[b * rows : (b + 1) * rows]).astype(BF)

    def pair_copy(h, j):
        line = line_of(h, j)
        src = work.at[0, line, :, 1 - c] if h == 0 else work.at[1, :, line, 1 - c]
        return remote(src, pair.at[h, j], pair_send.at[4 * h + j], pair_recv.at[4 * h + j], sibling)

    def line_copy(h, j):
        far = far_y if h == 0 else far_z
        device = at_place(x, (y + j) % 4, z, c) if h == 0 else at_place(x, y, (z + j) % 4, c)
        i = 3 * h + j - 1
        return remote(pair.at[h, j], far.at[j - 1], send_sem.at[i], recv_sem.at[i], device)

    def combine(h, j):
        pair_copy(h, j).wait_recv()
        line = line_of(h, j)

        @pl.loop(0, 4)
        def _(b):
            own = work[0, line, b, c] if h == 0 else work[1, b, line, c]
            pair[h, j, b] = (own.astype(F32) + pair[h, j, b].astype(F32)).astype(BF)

        if j:
            line_copy(h, j).start()

    lag = 2
    for i, (h, j) in enumerate(steps):
        load(h, j).wait()
        add_products(h, j)
        pair_copy(h, j).start()
        if i >= lag:
            combine(*steps[i - lag])
    for h, j in steps[-lag:]:
        combine(h, j)

    count = grad0_ref.shape[0]
    starts = [(2 * s + side) * count for s in (0, 1) for side in (t, 1 - t)]

    @pl.loop(0, feature_ref.shape[0] // TILE)
    def _(i):
        total = 0.0
        for start, piece in zip(starts, (grad0_ref, grad0_far_ref, grad1_ref)):
            hit = hits(rank_ref[tile_at(i)], start, count)
            total = total + jnp.dot(hit, piece[...], preferred_element_type=F32)
        feature_ref[tile_at(i)] = total.astype(BF)

    for h, j in steps:
        pair_copy(h, j).wait_send()

    def cross_copy(h, j):
        far = far_z2 if h == 0 else far_y2
        b = (z + j) % 4 if h == 0 else (y + j) % 4
        device = at_place(x, y, b, c) if h == 0 else at_place(x, b, z, c)
        i = 6 + 3 * h + j - 1
        return remote(pair.at[h, 0, b], far.at[j - 1], send_sem.at[i], recv_sem.at[i], device)

    for h in (0, 1):
        far = far_y if h == 0 else far_z
        for j in (2, 1, 3):
            line_copy(h, j).wait()

        @pl.loop(0, 4)
        def _(b, h=h, far=far):
            pair[h, 0, b] = (pair[h, 0, b].astype(F32) + far[0, b].astype(F32)
                             + far[1, b].astype(F32) + far[2, b].astype(F32)).astype(BF)

        for j in (2, 1, 3):
            cross_copy(h, j).start()

    back.wait()

    @pl.loop(0, feature_ref.shape[0] // TILE)
    def _(i):
        hit = hits(rank_ref[tile_at(i)], starts[3], count)
        found = jnp.dot(hit, grad1_far[...], preferred_element_type=F32)
        feature_ref[tile_at(i)] = (feature_ref[tile_at(i)].astype(F32) + found).astype(BF)

    for h in (0, 1):
        far = far_z2 if h == 0 else far_y2
        for j in (2, 1, 3):
            cross_copy(h, j).wait()
        mine = pair[h, 0, z] if h == 0 else pair[h, 0, y]
        stage[h] = (mine.astype(F32) + far[0].astype(F32) + far[1].astype(F32) + far[2].astype(F32)).astype(BF)

    def x_copy(j):
        device = (x + j) % 4
        i = 12 + j - 1
        return remote(stage.at[(device + x) % 2], far_x.at[j - 1], send_sem.at[i], recv_sem.at[i],
                      at_place(device, y, z, c))

    for j in (2, 1, 3):
        x_copy(j).start()
    for j in (2, 1, 3):
        x_copy(j).wait()
    total = (stage[0].astype(F32) + far_x[0].astype(F32) + far_x[1].astype(F32) + far_x[2].astype(F32)) * scale
    dino_ref[...] = total[:rows, : dino_ref.shape[1]]
    siglip_ref[...] = total[:rows, dino_ref.shape[1] :]


def finish(scale, part, turned, delta, delta_far, rank, grads, dino_cols):
    block = part.shape[-2:]
    count, features = grads[0].shape
    own_rows = features // 32
    return pl.pallas_call(
        functools.partial(tail_kernel, scale),
        out_shape=[
            jax.ShapeDtypeStruct((rank.shape[0], features), BF),
            jax.ShapeDtypeStruct((own_rows, dino_cols), F32),
            jax.ShapeDtypeStruct((own_rows, block[1] - dino_cols), F32)],
        in_specs=[HERE] + [VMEM] * 7,
        out_specs=[VMEM] * 3,
        scratch_shapes=[
            pltpu.VMEM((2, 4, 4, 2) + block, BF),
            pltpu.VMEM((2, 4, 4) + block, BF),
            pltpu.VMEM((3, 4) + block, BF),
            pltpu.VMEM((3, 4) + block, BF),
            pltpu.VMEM((3,) + block, BF),
            pltpu.VMEM((3,) + block, BF),
            pltpu.VMEM((3,) + block, BF),
            pltpu.VMEM((2,) + block, BF),
            pltpu.VMEM((count, features), BF),
            pltpu.SemaphoreType.DMA((8,)),
            pltpu.SemaphoreType.DMA((8,)),
            pltpu.SemaphoreType.DMA((8,)),
            pltpu.SemaphoreType.DMA((16,)),
            pltpu.SemaphoreType.DMA((16,)),
        ],
        compiler_params=pltpu.CompilerParams(
            collective_id=0, has_side_effects=True, vmem_limit_bytes=60 * 2**20
        ),
        cost_estimate=pl.CostEstimate(flops=10**10, bytes_accessed=5 * 10**7, transcendentals=0),
    )(part, turned, delta, delta_far, rank, *grads)


def per_device(student, dino_feat, siglip_feat, dino_weight, siglip_weight, send_index, recv_index):
    n_dp = lax.axis_size("dp")
    groups = n_dp * lax.axis_size("rep")
    row_count = student.shape[0]
    capacity = 2 * row_count // groups
    dino_cols = dino_feat.shape[1]
    t = lax.axis_index("tsec")
    rep = lax.axis_index("rep")
    swap = [(0, 1), (1, 0)]
    mirrored = [
        [((tt ^ r) * n_dp + d) * 2 + r for d in range(n_dp) for r in range(2)] for tt in range(2)
    ]

    own_rows = student.shape[1] // n_dp
    padded = -(-own_rows // 16) * 16

    def place_in(chunk, code):
        start, size = CHUNKS[chunk]
        slot = code % capacity - start
        return jnp.where((slot >= 0) & (slot < size), code // capacity * size + slot, -1)

    def exchange(outbox, chunk):
        arrived = lax.all_to_all(
            outbox.reshape(groups, CHUNKS[chunk][1], -1),
            ("tsec", "dp", "rep"),
            split_axis=0,
            concat_axis=0,
            axis_index_groups=mirrored,
            tiled=True,
        )
        return arrived.reshape(outbox.shape)

    outbox = fill_outbox(
        place_in(0, send_index)[None, :], dino_feat, siglip_feat.T, groups * CHUNKS[0][1], send_index)
    inbox = exchange(outbox, 0)

    key = (recv_index % capacity) * groups + recv_index // capacity
    rank = jnp.sum((key[:, None] > key[None, :]).astype(I32), 1)
    ranks = jnp.arange(row_count, dtype=I32)
    code_at = jnp.sum(jnp.where(rank[None, :] == ranks[:, None], recv_index[None, :], 0), 1)
    quarter = row_count // 4

    def columns_of(whose):
        codes, order = [
            jnp.concatenate([
                lax.dynamic_slice(values, ((2 * stage + whose) * quarter,), (quarter,)) for stage in (0, 1)
            ])
            for values in (code_at, ranks)
        ]
        direct = ((codes // capacity) % 2 == rep).astype(I32)
        return jnp.stack([order, direct] + [place_in(c, codes) for c in range(len(CHUNKS))], 1)

    columns, columns_far = columns_of(t), columns_of(1 - t)
    weights = [dino_weight, siglip_weight.T]
    normed, normed_bf, inv_dev, out, out_far, *weights_far, outbox = forward(
        columns, rank[None, :], place_in(1, send_index)[None, :], student, dino_feat, siglip_feat.T, weights,
        groups * CHUNKS[1][1], outbox)
    weights = weights + weights_far
    inboxes = [inbox, exchange(outbox, 1)]

    turned = normed_bf[quarter:].T
    by_z = turned.reshape(4, 4, -1, quarter).transpose(1, 0, 2, 3).reshape(turned.shape)
    turned = jnp.stack([turned, by_z])
    bases, grads = [], []
    for stage in (0, 1):
        delta, delta_far, grad, *bases = handle_block(
            stage, columns, columns_far, inv_dev, inboxes[stage], out, out_far, normed, weights, bases)
        grads.append(grad)
        if stage == 0:
            grads.append(lax.ppermute(grad, "tsec", swap))
            part = wgrad_part(normed_bf, [delta, delta_far], 0, n_dp, padded)
            bases = bases + [part]

    part = part.reshape((2, 4, 4, 2) + part.shape[2:])
    grad_scale = 1.0 / math.sqrt(row_count * groups)
    return tuple(finish(grad_scale, part, turned, delta, delta_far, rank[:, None], grads, dino_cols))


def solution(mesh):
    placed = (
        P(("dp", "rep"), None),
        P(("dp", "rep"), "tsec"),
        P(("dp", "rep"), "tsec"),
        P(None, "tsec"),
        P(None, "tsec"),
        P(("dp", "rep")),
        P(("dp", "rep")),
    )
    return jax.shard_map(
        per_device,
        mesh=mesh,
        in_specs=placed,
        out_specs=(P(("dp", "rep"), None), P("dp", "tsec"), P("dp", "tsec")),
        check_vma=False,
    )
```

```python
import functools
import math

import jax
import jax.numpy as jnp
from jax import lax
from jax.experimental import pallas as pl
from jax.experimental.pallas import tpu as pltpu
from jax.sharding import PartitionSpec as P

E1 = 1536
E2 = 1152
CHUNKS = ((0, 32), (32, 32))
TILE = 256

norm_eps = 1e-05
length_eps = 1e-06
MESH = pl.DeviceIdType.MESH
BF = jnp.bfloat16
F32 = jnp.float32
I32 = jnp.int32
HERE = pl.BlockSpec(memory_space=pl.ANY)
VMEM = pl.BlockSpec(memory_space=pltpu.VMEM)


def tile_of(rows):
    return next(size for size in (512, 384, 256, 128, 64, 32, 16) if rows % size == 0)


def whole(shape):
    return pl.BlockSpec(shape, lambda i: (0,) * len(shape), pipeline_mode=pl.Buffered(1))


def tiles(rows, width, first=0):
    return pl.BlockSpec((rows, width), lambda i: (first // rows + i, 0))


def local_call(kernel, steps, in_specs, out_specs, out_shape, *operands):
    return pl.pallas_call(
        kernel,
        grid=(steps,),
        in_specs=in_specs,
        out_specs=out_specs,
        out_shape=out_shape,
        compiler_params=pltpu.CompilerParams(vmem_limit_bytes=56 * 2**20),
        cost_estimate=pl.CostEstimate(flops=2**20, bytes_accessed=2**16, transcendentals=0),
    )(*operands)


def hits(column, first, count):
    return (column == first + lax.broadcasted_iota(I32, (column.shape[0], count), 1)).astype(BF)


def back_product(left_op, right_op):
    return lax.dot_general(
        left_op, right_op, (((1,), (1,)), ((), ())), preferred_element_type=F32
    )


def outbox_kernel(place_ref, dino_ref, siglip_ref, after_ref, out_ref):
    rows, count = out_ref.shape[0], dino_ref.shape[0]
    cols = dino_ref.shape[1]
    row = pl.program_id(0) * rows + lax.broadcasted_iota(I32, (rows, count), 0)
    hit = (row == place_ref[...]).astype(BF)
    out_ref[:, :cols] = jnp.dot(hit, dino_ref[...], preferred_element_type=F32).astype(BF)
    out_ref[:, cols:] = back_product(hit, siglip_ref[...]).astype(BF)


def fill_outbox(place, dino_feat, siglip_feat, rows, after):
    width = dino_feat.shape[1] + siglip_feat.shape[0]
    tile = tile_of(rows)
    return local_call(
        outbox_kernel, rows // tile,
        [whole((1, place.shape[1])), whole(dino_feat.shape), whole(siglip_feat.shape), HERE],
        tiles(tile, width), jax.ShapeDtypeStruct((rows, width), BF),
        place, dino_feat, siglip_feat, after)


def greet(devices):
    barrier = pltpu.get_barrier_semaphore()
    for device in devices:
        pl.semaphore_signal(barrier, inc=1, device_id=device, device_id_type=MESH)
    pl.semaphore_wait(barrier, len(devices))


def tile_at(i, start=0, tile=TILE):
    return pl.ds(pl.multiple_of(start + i * tile, tile), tile)


def remote(src, dst, send_sem, recv_sem, device):
    return pltpu.make_async_remote_copy(
        src_ref=src, dst_ref=dst, send_sem=send_sem, recv_sem=recv_sem, device_id=device, device_id_type=MESH)


def forward_kernel(columns_ref, rank_ref, place_ref, student_ref, dino_feat_ref, siglip_feat_ref, dino_ref, siglip_ref,
                   after_ref, normed_ref, bf_ref, inv_ref, out_ref, out_far_ref, dino_far_ref, siglip_far_ref,
                   outbox_ref, send_sem, recv_sem):
    dp, t = lax.axis_index("dp"), lax.axis_index("tsec")
    core = dp % 2
    partner, sibling = {"tsec": 1 - t}, {"dp": dp + 1 - 2 * core}
    greet([partner, sibling])
    cols = dino_ref.shape[1]

    fetches, swaps = [], []
    for i, (own, far) in enumerate(((dino_ref, dino_far_ref), (siglip_ref, siglip_far_ref))):
        size = own.shape[0] // 2
        part = pl.ds(pl.multiple_of(core * size, 16), size)
        fetches.append(remote(own.at[part], far.at[part], send_sem.at[i], recv_sem.at[i], partner))
        swaps.append(remote(far.at[part], far.at[part], send_sem.at[2 + i], recv_sem.at[2 + i], sibling))
    for copy in fetches:
        copy.start()

    @pl.loop(0, outbox_ref.shape[0] // TILE)
    def _(i):
        count = dino_feat_ref.shape[0]
        row = i * TILE + lax.broadcasted_iota(I32, (TILE, count), 0)
        hit = (row == place_ref[...]).astype(BF)
        outbox_ref[tile_at(i), :cols] = jnp.dot(hit, dino_feat_ref[...], preferred_element_type=F32).astype(BF)
        outbox_ref[tile_at(i), cols:] = back_product(hit, siglip_feat_ref[...]).astype(BF)

    @pl.loop(0, out_ref.shape[0] // TILE)
    def _(i):
        hit = (columns_ref[tile_at(i), 0:1] == rank_ref[...]).astype(BF)
        rows = jnp.dot(hit, student_ref[...], preferred_element_type=F32)
        centred = rows - jnp.mean(rows, 1, keepdims=True)
        inv_dev = lax.rsqrt(jnp.mean(centred * centred, 1, keepdims=True) + norm_eps)
        normed = centred * inv_dev
        normed_bf = normed.astype(BF)
        normed_ref[tile_at(i)] = normed
        bf_ref[tile_at(i)] = normed_bf
        inv_ref[tile_at(i)] = inv_dev
        out_ref[tile_at(i), :cols] = jnp.dot(normed_bf, dino_ref[...], preferred_element_type=F32)
        out_ref[tile_at(i), cols:] = back_product(normed_bf, siglip_ref[...])

    for copy, swap in zip(fetches, swaps):
        copy.wait_recv()
        swap.start()
    for swap in swaps:
        swap.wait_recv()

    @pl.loop(0, out_ref.shape[0] // TILE)
    def _(i):
        normed_bf = bf_ref[tile_at(i)]
        out_far_ref[tile_at(i), :cols] = jnp.dot(normed_bf, dino_far_ref[...], preferred_element_type=F32)
        out_far_ref[tile_at(i), cols:] = back_product(normed_bf, siglip_far_ref[...])

    for copy in fetches + swaps:
        copy.wait_send()


def forward(columns, rank, place, student, dino_feat, siglip_feat, weights, rows_out, after):
    rows, features = columns.shape[0], student.shape[1]
    width = weights[0].shape[1] + weights[1].shape[0]
    return pl.pallas_call(
        forward_kernel,
        in_specs=[VMEM] * 8 + [HERE],
        out_specs=[VMEM] * 8,
        out_shape=[
            jax.ShapeDtypeStruct((rows, features), F32), jax.ShapeDtypeStruct((rows, features), BF),
            jax.ShapeDtypeStruct((rows, 1), F32), jax.ShapeDtypeStruct((rows, width), F32),
            jax.ShapeDtypeStruct((rows, width), F32), jax.ShapeDtypeStruct(weights[0].shape, BF),
            jax.ShapeDtypeStruct(weights[1].shape, BF), jax.ShapeDtypeStruct((rows_out, width), BF)],
        scratch_shapes=[pltpu.SemaphoreType.DMA((4,)), pltpu.SemaphoreType.DMA((4,))],
        compiler_params=pltpu.CompilerParams(
            collective_id=1, has_side_effects=True, vmem_limit_bytes=60 * 2**20),
        cost_estimate=pl.CostEstimate(flops=3 * 10**10, bytes_accessed=5 * 10**7, transcendentals=0),
    )(columns, rank, place, student, dino_feat, siglip_feat, *weights, after)


def head_delta(outputs, targets, head_width):
    out_sq = sum(jnp.sum(y * y, 1, keepdims=True) for y in outputs)
    tgt_sq = sum(jnp.sum(f * f, 1, keepdims=True) for f in targets)
    cross = sum(jnp.sum(y * f, 1, keepdims=True) for y, f in zip(outputs, targets))
    out_len = jnp.sqrt(out_sq + length_eps)
    tgt_len = jnp.sqrt(tgt_sq + length_eps)
    cosine = cross / (out_len * tgt_len)
    pull_f = head_width / (out_len * tgt_len)
    pull_y = head_width * cosine / (out_len * out_len)
    return [
        (jnp.clip(y - f, -1.0, 1.0) - (pull_f * f - pull_y * y)).astype(BF)
        for y, f in zip(outputs, targets)
    ]


def block_kernel(stage, columns_ref, columns_far_ref, inv_ref, inbox_ref, out_ref, out_far_ref, normed_ref,
                 dino_ref, siglip_ref, dino_far_ref, siglip_far_ref, *refs):
    if stage == 0:
        delta_ref, delta_far_ref, grad_ref, base_far_ref, base_ref = refs[:5]
        refs = refs[5:]
    else:
        base_far_in, base_in, _, delta_ref, delta_far_ref, grad_ref = refs[:6]
        base_far_ref, base_ref = refs[-2:]
        refs = refs[6:-2]
    table, out, out_far, normed_all, dino_w, siglip_w, dino_far_w, siglip_far_w, sent, came, near_all = refs[:11]
    copy_sem, send_sem, recv_sem = refs[11:]
    rows = delta_ref.shape[0]
    first = stage * rows
    cols = dino_w.shape[1]
    tile = TILE // (1 + stage)
    at = functools.partial(tile_at, tile=tile)
    bases = ((base_far_in, base_far_ref), (base_in, base_ref)) if stage else ()
    loads = [
        pltpu.make_async_copy(src, dst, copy_sem.at[i])
        for i, (src, dst) in enumerate(((inbox_ref, table),) + bases + (
            (dino_ref, dino_w), (siglip_ref, siglip_w), (dino_far_ref, dino_far_w),
            (siglip_far_ref, siglip_far_w), (out_ref.at[pl.ds(first, rows)], out),
            (out_far_ref.at[pl.ds(first, rows)], out_far), (normed_ref.at[pl.ds(first, rows)], normed_all)))
    ]
    for load in loads:
        load.start()
    partner = {"tsec": 1 - lax.axis_index("tsec")}
    greet([partner])

    def swap(i):
        return remote(sent.at[at(i)], came.at[at(i)], send_sem.at[i], recv_sem.at[i], partner)

    def look_up(column):
        hit = (column == lax.broadcasted_iota(I32, (tile, table.shape[0]), 1)).astype(BF)
        return jnp.dot(hit, table[...], preferred_element_type=F32)

    for load in loads[: 1 + len(bases)]:
        load.wait()
    steps = rows // tile
    for i in range(steps):
        found = look_up(columns_far_ref[at(i, first), 2 + stage : 3 + stage])
        if stage:
            found = found + base_far_ref[at(i)].astype(F32)
        sent[at(i)] = found.astype(BF)
        swap(i).start()
    for i in range(steps):
        found = look_up(columns_ref[at(i, first), 2 + stage : 3 + stage])
        if stage:
            found = found + base_ref[at(i)].astype(F32)
        near_all[at(i)] = found.astype(BF)
    if stage == 0:
        for i in range(steps):
            base_far_ref[at(i)] = look_up(columns_far_ref[at(i, rows), 2:3]).astype(BF)
            base_ref[at(i)] = look_up(columns_ref[at(i, rows), 2:3]).astype(BF)
    for load in loads[1 + len(bases) :]:
        load.wait()
    for i in range(steps):
        swap(i).wait_recv()
        near, far = near_all[at(i)].astype(F32), came[at(i)].astype(F32)
        direct = columns_ref[at(i, first), 1:2] > 0
        own = jnp.where(direct, near, far)
        other = jnp.where(direct, far, near)
        y, y_far = out[at(i)], out_far[at(i)]
        dino = head_delta([y[:, :cols], y_far[:, :cols]], [own[:, :cols], other[:, :cols]], float(E1))
        siglip = head_delta([y[:, cols:], y_far[:, cols:]], [own[:, cols:], other[:, cols:]], float(E2))
        for delta, d, g in ((delta_ref, dino[0], siglip[0]), (delta_far_ref, dino[1], siglip[1])):
            delta[at(i), :cols] = d
            delta[at(i), cols:] = g
        part = back_product(dino[0], dino_w[...]) + jnp.dot(siglip[0], siglip_w[...], preferred_element_type=F32)
        part_far = back_product(dino[1], dino_far_w[...]) + jnp.dot(
            siglip[1], siglip_far_w[...], preferred_element_type=F32)
        normed_grad = part.astype(BF).astype(F32) + part_far.astype(BF).astype(F32)
        normed = normed_all[at(i)]
        grad_mean = jnp.mean(normed_grad, 1, keepdims=True)
        grad_proj = jnp.mean(normed_grad * normed, 1, keepdims=True)
        inv_dev = inv_ref[at(i, first)]
        grad_ref[at(i)] = ((normed_grad - grad_mean - normed * grad_proj) * inv_dev).astype(BF)
    for i in range(steps):
        swap(i).wait_send()


def handle_block(stage, columns, columns_far, inv_dev, inbox, out, out_far, normed, weights, bases):
    rows, features = normed.shape[0] // 2, normed.shape[1]
    width = inbox.shape[1]
    wide, thin = jax.ShapeDtypeStruct((rows, width), BF), jax.ShapeDtypeStruct((rows, features), BF)
    shapes = [wide, wide, thin] + ([wide, wide] if stage == 0 else [])
    steps = rows // TILE * (1 + stage)
    return pl.pallas_call(
        functools.partial(block_kernel, stage),
        in_specs=[VMEM] * 3 + [HERE] * (11 if stage else 8),
        out_specs=[VMEM] * len(shapes),
        out_shape=shapes,
        scratch_shapes=[
            pltpu.VMEM(inbox.shape, BF), pltpu.VMEM((rows, width), F32), pltpu.VMEM((rows, width), F32),
            pltpu.VMEM((rows, features), F32)] + [pltpu.VMEM(w.shape, BF) for w in weights] + [
            pltpu.VMEM((rows, width), BF), pltpu.VMEM((rows, width), BF), pltpu.VMEM((rows, width), BF),
            pltpu.SemaphoreType.DMA((10,)), pltpu.SemaphoreType.DMA((steps,)), pltpu.SemaphoreType.DMA((steps,))]
        + [pltpu.VMEM((rows, width), BF) for _ in range(2 * stage)],
        compiler_params=pltpu.CompilerParams(
            collective_id=2 + stage, has_side_effects=True, vmem_limit_bytes=60 * 2**20),
        cost_estimate=pl.CostEstimate(flops=10**10, bytes_accessed=3 * 10**7, transcendentals=0),
    )(columns, columns_far, inv_dev, inbox, out, out_far, normed, *weights, *bases)


def wgrad_kernel(n, bf_ref, *refs):
    deltas, base, part_ref = refs[:n], refs[n:-1], refs[-1]
    blocks, rows = part_ref.shape[1], bf_ref.shape[1] // part_ref.shape[1]
    for side in (0, 1):
        total, start = 0.0, 0
        for delta in deltas[side::2]:
            size = delta.shape[0]
            total = total + lax.dot_general(
                bf_ref[start : start + size], delta[...], (((0,), (0,)), ((), ())), preferred_element_type=F32)
            start += size
        for b in range(blocks):
            value = total[b * rows : (b + 1) * rows]
            if base:
                value = value + base[0][side, b, :rows].astype(F32)
            part_ref[side, b, :rows] = value.astype(BF)
            part_ref[side, b, rows:] = jnp.zeros((part_ref.shape[2] - rows, part_ref.shape[3]), BF)


def wgrad_part(normed_bf, deltas, first, owners, padded, base=None):
    features = normed_bf.shape[1]
    rows = sum(d.shape[0] for d in deltas[::2])
    width = deltas[0].shape[1]
    split = 2
    blocks = pl.BlockSpec((2, owners // split, padded, width), lambda i: (0, i, 0, 0))
    more = [] if base is None else [base]
    return pl.pallas_call(
        functools.partial(wgrad_kernel, len(deltas)),
        grid=(split,),
        in_specs=[pl.BlockSpec((rows, features // split), lambda i: (first // rows, i))]
        + [whole(d.shape) for d in deltas] + [blocks for _ in more],
        out_specs=blocks,
        out_shape=jax.ShapeDtypeStruct((2, owners, padded, width), BF),
        compiler_params=pltpu.CompilerParams(vmem_limit_bytes=58 * 2**20),
        cost_estimate=pl.CostEstimate(flops=2**20, bytes_accessed=2**16, transcendentals=0),
    )(normed_bf, *deltas, *more)


def place():
    dp = lax.axis_index("dp")
    x = lax.axis_index("rep") * 2 + lax.axis_index("tsec")
    return x, dp // 8, (dp // 2) % 4, dp % 2


def at_place(x, y, z, c):
    return {"tsec": x % 2, "dp": (y * 4 + z) * 2 + c, "rep": x // 2}


def tail_kernel(scale, part_ref, turned_ref, delta_ref, delta_far_ref, rank_ref, grad0_in, grad0_far_in, grad1_in,
                feature_out, dino_ref, siglip_ref,
                work, pair, far_y, far_z, far_y2, far_z2, far_x, stage, grad1_far,
                load_sem, pair_send, pair_recv, send_sem, recv_sem,
                feature_ref, grad0_ref, grad0_far_ref, grad1_ref, grad_sem, out_sem):
    x, y, z, c = place()
    t = x % 2
    sibling, partner = at_place(x, y, z, 1 - c), {"tsec": 1 - t}
    steps = [(h, j) for j in (2, 1, 3, 0) for h in (0, 1)]

    def line_of(h, j):
        return (y + j) % 4 if h == 0 else (z + j) % 4

    def load(h, j):
        line = line_of(h, j)
        src, dst = (r.at[0, line] if h == 0 else r.at[1, :, line] for r in (part_ref, work))
        return pltpu.make_async_copy(src, dst, load_sem.at[4 * h + j])

    for h, j in steps:
        load(h, j).start()
    grad_loads = [
        pltpu.make_async_copy(src, dst, grad_sem.at[i])
        for i, (src, dst) in enumerate(
            ((grad0_in, grad0_ref), (grad0_far_in, grad0_far_ref), (grad1_in, grad1_ref)))]
    for copy in grad_loads:
        copy.start()

    def store(i):
        return pltpu.make_async_copy(feature_ref.at[tile_at(i)], feature_out.at[tile_at(i)], out_sem.at[i])

    lines = [[at_place(x, (y + j) % 4, z, c), at_place(x, y, (z + j) % 4, c), at_place((x + j) % 4, y, z, c)]
             for j in (1, 2, 3)]
    greet([sibling] + sum(lines, []))
    back = remote(grad1_in, grad1_far, send_sem.at[15], recv_sem.at[15], partner)
    back.start()
    rows = feature_ref.shape[1] // 32

    def add_products(h, j):
        delta = delta_ref if h == 0 else delta_far_ref
        line = line_of(h, j)
        features = pl.ds(pl.multiple_of(line * 8 * rows, 16), 8 * rows)
        new = jnp.dot(turned_ref[h, features], delta[...], preferred_element_type=F32)
        for b in range(8):
            at = (0, line, b // 2, b % 2) if h == 0 else (1, b // 2, line, b % 2)
            old = work[at + (slice(0, rows),)].astype(F32)
            work[at + (slice(0, rows),)] = (old + new[b * rows : (b + 1) * rows]).astype(BF)

    def pair_copy(h, j):
        line = line_of(h, j)
        src = work.at[0, line, :, 1 - c] if h == 0 else work.at[1, :, line, 1 - c]
        return remote(src, pair.at[h, j], pair_send.at[4 * h + j], pair_recv.at[4 * h + j], sibling)

    def line_copy(h, j):
        far = far_y if h == 0 else far_z
        device = at_place(x, (y + j) % 4, z, c) if h == 0 else at_place(x, y, (z + j) % 4, c)
        i = 3 * h + j - 1
        return remote(pair.at[h, j], far.at[j - 1], send_sem.at[i], recv_sem.at[i], device)

    def combine(h, j):
        pair_copy(h, j).wait_recv()
        line = line_of(h, j)

        @pl.loop(0, 4)
        def _(b):
            own = work[0, line, b, c] if h == 0 else work[1, b, line, c]
            pair[h, j, b] = (own.astype(F32) + pair[h, j, b].astype(F32)).astype(BF)

        if j:
            line_copy(h, j).start()

    lag = 2
    for i, (h, j) in enumerate(steps):
        load(h, j).wait()
        add_products(h, j)
        pair_copy(h, j).start()
        if i >= lag:
            combine(*steps[i - lag])
    for h, j in steps[-lag:]:
        combine(h, j)

    for copy in grad_loads:
        copy.wait()

    count = grad0_ref.shape[0]
    starts = [(2 * s + side) * count for s in (0, 1) for side in (t, 1 - t)]

    @pl.loop(0, feature_ref.shape[0] // TILE)
    def _(i):
        total = 0.0
        for start, piece in zip(starts, (grad0_ref, grad0_far_ref, grad1_ref)):
            hit = hits(rank_ref[tile_at(i)], start, count)
            total = total + jnp.dot(hit, piece[...], preferred_element_type=F32)
        feature_ref[tile_at(i)] = total.astype(BF)

    for h, j in steps:
        pair_copy(h, j).wait_send()

    def cross_copy(h, j):
        far = far_z2 if h == 0 else far_y2
        b = (z + j) % 4 if h == 0 else (y + j) % 4
        device = at_place(x, y, b, c) if h == 0 else at_place(x, b, z, c)
        i = 6 + 3 * h + j - 1
        return remote(pair.at[h, 0, b], far.at[j - 1], send_sem.at[i], recv_sem.at[i], device)

    for h in (0, 1):
        far = far_y if h == 0 else far_z
        for j in (2, 1, 3):
            line_copy(h, j).wait()

        @pl.loop(0, 4)
        def _(b, h=h, far=far):
            pair[h, 0, b] = (pair[h, 0, b].astype(F32) + far[0, b].astype(F32)
                             + far[1, b].astype(F32) + far[2, b].astype(F32)).astype(BF)

        for j in (2, 1, 3):
            cross_copy(h, j).start()

    back.wait()

    @pl.loop(0, feature_ref.shape[0] // TILE)
    def _(i):
        hit = hits(rank_ref[tile_at(i)], starts[3], count)
        found = jnp.dot(hit, grad1_far[...], preferred_element_type=F32)
        feature_ref[tile_at(i)] = (feature_ref[tile_at(i)].astype(F32) + found).astype(BF)
        store(i).start()

    for h in (0, 1):
        far = far_z2 if h == 0 else far_y2
        for j in (2, 1, 3):
            cross_copy(h, j).wait()
        mine = pair[h, 0, z] if h == 0 else pair[h, 0, y]
        stage[h] = (mine.astype(F32) + far[0].astype(F32) + far[1].astype(F32) + far[2].astype(F32)).astype(BF)

    def x_copy(j):
        device = (x + j) % 4
        i = 12 + j - 1
        return remote(stage.at[(device + x) % 2], far_x.at[j - 1], send_sem.at[i], recv_sem.at[i],
                      at_place(device, y, z, c))

    for j in (2, 1, 3):
        x_copy(j).start()
    for j in (2, 1, 3):
        x_copy(j).wait()
    total = (stage[0].astype(F32) + far_x[0].astype(F32) + far_x[1].astype(F32) + far_x[2].astype(F32)) * scale
    @pl.loop(0, feature_ref.shape[0] // TILE)
    def _(i):
        store(i).wait()

    dino_ref[...] = total[:rows, : dino_ref.shape[1]]
    siglip_ref[...] = total[:rows, dino_ref.shape[1] :]


def finish(scale, part, turned, delta, delta_far, rank, grads, dino_cols):
    block = part.shape[-2:]
    count, features = grads[0].shape
    own_rows = features // 32
    return pl.pallas_call(
        functools.partial(tail_kernel, scale),
        out_shape=[
            jax.ShapeDtypeStruct((rank.shape[0], features), BF),
            jax.ShapeDtypeStruct((own_rows, dino_cols), F32),
            jax.ShapeDtypeStruct((own_rows, block[1] - dino_cols), F32)],
        in_specs=[HERE] + [VMEM] * 4 + [HERE] * 3,
        out_specs=[HERE] + [VMEM] * 2,
        scratch_shapes=[
            pltpu.VMEM((2, 4, 4, 2) + block, BF),
            pltpu.VMEM((2, 4, 4) + block, BF),
            pltpu.VMEM((3, 4) + block, BF),
            pltpu.VMEM((3, 4) + block, BF),
            pltpu.VMEM((3,) + block, BF),
            pltpu.VMEM((3,) + block, BF),
            pltpu.VMEM((3,) + block, BF),
            pltpu.VMEM((2,) + block, BF),
            pltpu.VMEM((count, features), BF),
            pltpu.SemaphoreType.DMA((8,)),
            pltpu.SemaphoreType.DMA((8,)),
            pltpu.SemaphoreType.DMA((8,)),
            pltpu.SemaphoreType.DMA((16,)),
            pltpu.SemaphoreType.DMA((16,)),
            pltpu.VMEM((rank.shape[0], features), BF),
        ]
        + [pltpu.VMEM((count, features), BF)] * 3
        + [pltpu.SemaphoreType.DMA((3,)), pltpu.SemaphoreType.DMA((rank.shape[0] // TILE,))],
        compiler_params=pltpu.CompilerParams(
            collective_id=0, has_side_effects=True, vmem_limit_bytes=60 * 2**20
        ),
        cost_estimate=pl.CostEstimate(flops=10**10, bytes_accessed=5 * 10**7, transcendentals=0),
    )(part, turned, delta, delta_far, rank, *grads)


def per_device(student, dino_feat, siglip_feat, dino_weight, siglip_weight, send_index, recv_index):
    n_dp = lax.axis_size("dp")
    groups = n_dp * lax.axis_size("rep")
    row_count = student.shape[0]
    capacity = 2 * row_count // groups
    dino_cols = dino_feat.shape[1]
    t = lax.axis_index("tsec")
    rep = lax.axis_index("rep")
    swap = [(0, 1), (1, 0)]
    mirrored = [
        [((tt ^ r) * n_dp + d) * 2 + r for d in range(n_dp) for r in range(2)] for tt in range(2)
    ]

    own_rows = student.shape[1] // n_dp
    padded = -(-own_rows // 16) * 16

    def place_in(chunk, code):
        start, size = CHUNKS[chunk]
        slot = code % capacity - start
        return jnp.where((slot >= 0) & (slot < size), code // capacity * size + slot, -1)

    def exchange(outbox, chunk):
        arrived = lax.all_to_all(
            outbox.reshape(groups, CHUNKS[chunk][1], -1),
            ("tsec", "dp", "rep"),
            split_axis=0,
            concat_axis=0,
            axis_index_groups=mirrored,
            tiled=True,
        )
        return arrived.reshape(outbox.shape)

    outbox = fill_outbox(
        place_in(0, send_index)[None, :], dino_feat, siglip_feat.T, groups * CHUNKS[0][1], send_index)
    inbox = exchange(outbox, 0)

    key = (recv_index % capacity) * groups + recv_index // capacity
    rank = jnp.sum((key[:, None] > key[None, :]).astype(I32), 1)
    ranks = jnp.arange(row_count, dtype=I32)
    code_at = jnp.sum(jnp.where(rank[None, :] == ranks[:, None], recv_index[None, :], 0), 1)
    quarter = row_count // 4

    def columns_of(whose):
        codes, order = [
            jnp.concatenate([
                lax.dynamic_slice(values, ((2 * stage + whose) * quarter,), (quarter,)) for stage in (0, 1)
            ])
            for values in (code_at, ranks)
        ]
        direct = ((codes // capacity) % 2 == rep).astype(I32)
        return jnp.stack([order, direct] + [place_in(c, codes) for c in range(len(CHUNKS))], 1)

    columns, columns_far = columns_of(t), columns_of(1 - t)
    weights = [dino_weight, siglip_weight.T]
    normed, normed_bf, inv_dev, out, out_far, *weights_far, outbox = forward(
        columns, rank[None, :], place_in(1, send_index)[None, :], student, dino_feat, siglip_feat.T, weights,
        groups * CHUNKS[1][1], outbox)
    weights = weights + weights_far
    inboxes = [inbox, exchange(outbox, 1)]

    turned = normed_bf[quarter:].T
    by_z = turned.reshape(4, 4, -1, quarter).transpose(1, 0, 2, 3).reshape(turned.shape)
    turned = jnp.stack([turned, by_z])
    bases, grads = [], []
    for stage in (0, 1):
        delta, delta_far, grad, *bases = handle_block(
            stage, columns, columns_far, inv_dev, inboxes[stage], out, out_far, normed, weights, bases)
        grads.append(grad)
        if stage == 0:
            grads.append(lax.ppermute(grad, "tsec", swap))
            part = wgrad_part(normed_bf, [delta, delta_far], 0, n_dp, padded)
            bases = bases + [part]

    part = part.reshape((2, 4, 4, 2) + part.shape[2:])
    grad_scale = 1.0 / math.sqrt(row_count * groups)
    return tuple(finish(grad_scale, part, turned, delta, delta_far, rank[:, None], grads, dino_cols))


def solution(mesh):
    placed = (
        P(("dp", "rep"), None),
        P(("dp", "rep"), "tsec"),
        P(("dp", "rep"), "tsec"),
        P(None, "tsec"),
        P(None, "tsec"),
        P(("dp", "rep")),
        P(("dp", "rep")),
    )
    return jax.shard_map(
        per_device,
        mesh=mesh,
        in_specs=placed,
        out_specs=(P(("dp", "rep"), None), P("dp", "tsec"), P("dp", "tsec")),
        check_vma=False,
    )
```

```python
import functools
import math

import jax
import jax.numpy as jnp
from jax import lax
from jax.experimental import pallas as pl
from jax.experimental.pallas import tpu as pltpu
from jax.sharding import PartitionSpec as P

E1 = 1536
E2 = 1152
CHUNKS = ((0, 32), (32, 32))
TILE = 256

norm_eps = 1e-05
length_eps = 1e-06
MESH = pl.DeviceIdType.MESH
BF = jnp.bfloat16
F32 = jnp.float32
I32 = jnp.int32
HERE = pl.BlockSpec(memory_space=pl.ANY)
VMEM = pl.BlockSpec(memory_space=pltpu.VMEM)


def tile_of(rows):
    return next(size for size in (512, 384, 256, 128, 64, 32, 16) if rows % size == 0)


def whole(shape):
    return pl.BlockSpec(shape, lambda i: (0,) * len(shape), pipeline_mode=pl.Buffered(1))


def tiles(rows, width, first=0):
    return pl.BlockSpec((rows, width), lambda i: (first // rows + i, 0))


def local_call(kernel, steps, in_specs, out_specs, out_shape, *operands):
    return pl.pallas_call(
        kernel,
        grid=(steps,),
        in_specs=in_specs,
        out_specs=out_specs,
        out_shape=out_shape,
        compiler_params=pltpu.CompilerParams(vmem_limit_bytes=56 * 2**20),
        cost_estimate=pl.CostEstimate(flops=2**20, bytes_accessed=2**16, transcendentals=0),
    )(*operands)


def hits(column, first, count):
    return (column == first + lax.broadcasted_iota(I32, (column.shape[0], count), 1)).astype(BF)


def back_product(left_op, right_op):
    return lax.dot_general(
        left_op, right_op, (((1,), (1,)), ((), ())), preferred_element_type=F32
    )


def outbox_kernel(place_ref, dino_ref, siglip_ref, after_ref, out_ref):
    rows, count = out_ref.shape[0], dino_ref.shape[0]
    cols = dino_ref.shape[1]
    row = pl.program_id(0) * rows + lax.broadcasted_iota(I32, (rows, count), 0)
    hit = (row == place_ref[...]).astype(BF)
    out_ref[:, :cols] = jnp.dot(hit, dino_ref[...], preferred_element_type=F32).astype(BF)
    out_ref[:, cols:] = back_product(hit, siglip_ref[...]).astype(BF)


def fill_outbox(place, dino_feat, siglip_feat, rows, after):
    width = dino_feat.shape[1] + siglip_feat.shape[0]
    tile = tile_of(rows)
    return local_call(
        outbox_kernel, rows // tile,
        [whole((1, place.shape[1])), whole(dino_feat.shape), whole(siglip_feat.shape), HERE],
        tiles(tile, width), jax.ShapeDtypeStruct((rows, width), BF),
        place, dino_feat, siglip_feat, after)


def greet(devices):
    barrier = pltpu.get_barrier_semaphore()
    for device in devices:
        pl.semaphore_signal(barrier, inc=1, device_id=device, device_id_type=MESH)
    pl.semaphore_wait(barrier, len(devices))


def tile_at(i, start=0, tile=TILE):
    return pl.ds(pl.multiple_of(start + i * tile, tile), tile)


def remote(src, dst, send_sem, recv_sem, device):
    return pltpu.make_async_remote_copy(
        src_ref=src, dst_ref=dst, send_sem=send_sem, recv_sem=recv_sem, device_id=device, device_id_type=MESH)


def forward_kernel(columns_ref, rank_ref, place_ref, student_ref, dino_feat_ref, siglip_feat_ref, dino_ref, siglip_ref,
                   after_ref, normed_ref, bf_ref, inv_ref, out_ref, out_far_ref, dino_far_ref, siglip_far_ref,
                   outbox_ref, send_sem, recv_sem):
    dp, t = lax.axis_index("dp"), lax.axis_index("tsec")
    core = dp % 2
    partner, sibling = {"tsec": 1 - t}, {"dp": dp + 1 - 2 * core}
    greet([partner, sibling])
    cols = dino_ref.shape[1]

    fetches, swaps = [], []
    for i, (own, far) in enumerate(((dino_ref, dino_far_ref), (siglip_ref, siglip_far_ref))):
        size = own.shape[0] // 2
        part = pl.ds(pl.multiple_of(core * size, 16), size)
        fetches.append(remote(own.at[part], far.at[part], send_sem.at[i], recv_sem.at[i], partner))
        swaps.append(remote(far.at[part], far.at[part], send_sem.at[2 + i], recv_sem.at[2 + i], sibling))
    for copy in fetches:
        copy.start()

    @pl.loop(0, outbox_ref.shape[0] // TILE)
    def _(i):
        count = dino_feat_ref.shape[0]
        row = i * TILE + lax.broadcasted_iota(I32, (TILE, count), 0)
        hit = (row == place_ref[...]).astype(BF)
        outbox_ref[tile_at(i), :cols] = jnp.dot(hit, dino_feat_ref[...], preferred_element_type=F32).astype(BF)
        outbox_ref[tile_at(i), cols:] = back_product(hit, siglip_feat_ref[...]).astype(BF)

    @pl.loop(0, out_ref.shape[0] // TILE)
    def _(i):
        hit = (columns_ref[tile_at(i), 0:1] == rank_ref[...]).astype(BF)
        rows = jnp.dot(hit, student_ref[...], preferred_element_type=F32)
        centred = rows - jnp.mean(rows, 1, keepdims=True)
        inv_dev = lax.rsqrt(jnp.mean(centred * centred, 1, keepdims=True) + norm_eps)
        normed = centred * inv_dev
        normed_bf = normed.astype(BF)
        normed_ref[tile_at(i)] = normed
        bf_ref[tile_at(i)] = normed_bf
        inv_ref[tile_at(i)] = inv_dev
        out_ref[tile_at(i), :cols] = jnp.dot(normed_bf, dino_ref[...], preferred_element_type=F32)
        out_ref[tile_at(i), cols:] = back_product(normed_bf, siglip_ref[...])

    for copy, swap in zip(fetches, swaps):
        copy.wait_recv()
        swap.start()
    for swap in swaps:
        swap.wait_recv()

    @pl.loop(0, out_ref.shape[0] // TILE)
    def _(i):
        normed_bf = bf_ref[tile_at(i)]
        out_far_ref[tile_at(i), :cols] = jnp.dot(normed_bf, dino_far_ref[...], preferred_element_type=F32)
        out_far_ref[tile_at(i), cols:] = back_product(normed_bf, siglip_far_ref[...])

    for copy in fetches + swaps:
        copy.wait_send()


def forward(columns, rank, place, student, dino_feat, siglip_feat, weights, rows_out, after):
    rows, features = columns.shape[0], student.shape[1]
    width = weights[0].shape[1] + weights[1].shape[0]
    return pl.pallas_call(
        forward_kernel,
        in_specs=[VMEM] * 8 + [HERE],
        out_specs=[VMEM] * 8,
        out_shape=[
            jax.ShapeDtypeStruct((rows, features), F32), jax.ShapeDtypeStruct((rows, features), BF),
            jax.ShapeDtypeStruct((rows, 1), F32), jax.ShapeDtypeStruct((rows, width), F32),
            jax.ShapeDtypeStruct((rows, width), F32), jax.ShapeDtypeStruct(weights[0].shape, BF),
            jax.ShapeDtypeStruct(weights[1].shape, BF), jax.ShapeDtypeStruct((rows_out, width), BF)],
        scratch_shapes=[pltpu.SemaphoreType.DMA((4,)), pltpu.SemaphoreType.DMA((4,))],
        compiler_params=pltpu.CompilerParams(
            collective_id=1, has_side_effects=True, vmem_limit_bytes=60 * 2**20),
        cost_estimate=pl.CostEstimate(flops=3 * 10**10, bytes_accessed=5 * 10**7, transcendentals=0),
    )(columns, rank, place, student, dino_feat, siglip_feat, *weights, after)


def head_delta(outputs, targets, head_width):
    out_sq = sum(jnp.sum(y * y, 1, keepdims=True) for y in outputs)
    tgt_sq = sum(jnp.sum(f * f, 1, keepdims=True) for f in targets)
    cross = sum(jnp.sum(y * f, 1, keepdims=True) for y, f in zip(outputs, targets))
    out_len = jnp.sqrt(out_sq + length_eps)
    tgt_len = jnp.sqrt(tgt_sq + length_eps)
    cosine = cross / (out_len * tgt_len)
    pull_f = head_width / (out_len * tgt_len)
    pull_y = head_width * cosine / (out_len * out_len)
    return [
        (jnp.clip(y - f, -1.0, 1.0) - (pull_f * f - pull_y * y)).astype(BF)
        for y, f in zip(outputs, targets)
    ]


def block_kernel(stage, columns_ref, columns_far_ref, inv_ref, inbox_ref, out_ref, out_far_ref, normed_ref,
                 dino_ref, siglip_ref, dino_far_ref, siglip_far_ref, *refs):
    if stage == 0:
        delta_ref, delta_far_ref, grad_ref, base_far_ref, base_ref = refs[:5]
        refs = refs[5:]
    else:
        base_far_in, base_in, _, delta_ref, delta_far_ref, grad_ref = refs[:6]
        base_far_ref, base_ref = refs[-2:]
        refs = refs[6:-2]
    table, out, out_far, normed_all, dino_w, siglip_w, dino_far_w, siglip_far_w, sent, came, near_all = refs[:11]
    copy_sem, send_sem, recv_sem = refs[11:]
    rows = delta_ref.shape[0]
    first = stage * rows
    cols = dino_w.shape[1]
    tile = TILE // (1 + stage)
    at = functools.partial(tile_at, tile=tile)
    bases = ((base_far_in, base_far_ref), (base_in, base_ref)) if stage else ()
    loads = [
        pltpu.make_async_copy(src, dst, copy_sem.at[i])
        for i, (src, dst) in enumerate(((inbox_ref, table),) + bases + (
            (dino_ref, dino_w), (siglip_ref, siglip_w), (dino_far_ref, dino_far_w),
            (siglip_far_ref, siglip_far_w), (out_ref.at[pl.ds(first, rows)], out),
            (out_far_ref.at[pl.ds(first, rows)], out_far), (normed_ref.at[pl.ds(first, rows)], normed_all)))
    ]
    for load in loads[: 1 + len(bases)]:
        load.start()
    partner = {"tsec": 1 - lax.axis_index("tsec")}
    greet([partner])

    def swap(i):
        return remote(sent.at[at(i)], came.at[at(i)], send_sem.at[i], recv_sem.at[i], partner)

    def look_up(column):
        hit = (column == lax.broadcasted_iota(I32, (tile, table.shape[0]), 1)).astype(BF)
        return jnp.dot(hit, table[...], preferred_element_type=F32)

    for load in loads[: 1 + len(bases)]:
        load.wait()
    for load in loads[1 + len(bases) :]:
        load.start()
    steps = rows // tile
    for i in range(steps):
        found = look_up(columns_far_ref[at(i, first), 2 + stage : 3 + stage])
        if stage:
            found = found + base_far_ref[at(i)].astype(F32)
        sent[at(i)] = found.astype(BF)
        swap(i).start()
    for i in range(steps):
        found = look_up(columns_ref[at(i, first), 2 + stage : 3 + stage])
        if stage:
            found = found + base_ref[at(i)].astype(F32)
        near_all[at(i)] = found.astype(BF)
    if stage == 0:
        for i in range(steps):
            base_far_ref[at(i)] = look_up(columns_far_ref[at(i, rows), 2:3]).astype(BF)
            base_ref[at(i)] = look_up(columns_ref[at(i, rows), 2:3]).astype(BF)
    for load in loads[1 + len(bases) :]:
        load.wait()
    for i in range(steps):
        swap(i).wait_recv()
        near, far = near_all[at(i)].astype(F32), came[at(i)].astype(F32)
        direct = columns_ref[at(i, first), 1:2] > 0
        own = jnp.where(direct, near, far)
        other = jnp.where(direct, far, near)
        y, y_far = out[at(i)], out_far[at(i)]
        dino = head_delta([y[:, :cols], y_far[:, :cols]], [own[:, :cols], other[:, :cols]], float(E1))
        siglip = head_delta([y[:, cols:], y_far[:, cols:]], [own[:, cols:], other[:, cols:]], float(E2))
        for delta, d, g in ((delta_ref, dino[0], siglip[0]), (delta_far_ref, dino[1], siglip[1])):
            delta[at(i), :cols] = d
            delta[at(i), cols:] = g
        part = back_product(dino[0], dino_w[...]) + jnp.dot(siglip[0], siglip_w[...], preferred_element_type=F32)
        part_far = back_product(dino[1], dino_far_w[...]) + jnp.dot(
            siglip[1], siglip_far_w[...], preferred_element_type=F32)
        normed_grad = part.astype(BF).astype(F32) + part_far.astype(BF).astype(F32)
        normed = normed_all[at(i)]
        grad_mean = jnp.mean(normed_grad, 1, keepdims=True)
        grad_proj = jnp.mean(normed_grad * normed, 1, keepdims=True)
        inv_dev = inv_ref[at(i, first)]
        grad_ref[at(i)] = ((normed_grad - grad_mean - normed * grad_proj) * inv_dev).astype(BF)
    for i in range(steps):
        swap(i).wait_send()


def handle_block(stage, columns, columns_far, inv_dev, inbox, out, out_far, normed, weights, bases):
    rows, features = normed.shape[0] // 2, normed.shape[1]
    width = inbox.shape[1]
    wide, thin = jax.ShapeDtypeStruct((rows, width), BF), jax.ShapeDtypeStruct((rows, features), BF)
    shapes = [wide, wide, thin] + ([wide, wide] if stage == 0 else [])
    steps = rows // TILE * (1 + stage)
    return pl.pallas_call(
        functools.partial(block_kernel, stage),
        in_specs=[VMEM] * 3 + [HERE] * (11 if stage else 8),
        out_specs=[VMEM] * len(shapes),
        out_shape=shapes,
        scratch_shapes=[
            pltpu.VMEM(inbox.shape, BF), pltpu.VMEM((rows, width), F32), pltpu.VMEM((rows, width), F32),
            pltpu.VMEM((rows, features), F32)] + [pltpu.VMEM(w.shape, BF) for w in weights] + [
            pltpu.VMEM((rows, width), BF), pltpu.VMEM((rows, width), BF), pltpu.VMEM((rows, width), BF),
            pltpu.SemaphoreType.DMA((10,)), pltpu.SemaphoreType.DMA((steps,)), pltpu.SemaphoreType.DMA((steps,))]
        + [pltpu.VMEM((rows, width), BF) for _ in range(2 * stage)],
        compiler_params=pltpu.CompilerParams(
            collective_id=2 + stage, has_side_effects=True, vmem_limit_bytes=60 * 2**20),
        cost_estimate=pl.CostEstimate(flops=10**10, bytes_accessed=3 * 10**7, transcendentals=0),
    )(columns, columns_far, inv_dev, inbox, out, out_far, normed, *weights, *bases)


def wgrad_kernel(n, bf_ref, *refs):
    deltas, base, part_ref = refs[:n], refs[n:-1], refs[-1]
    blocks, rows = part_ref.shape[1], bf_ref.shape[1] // part_ref.shape[1]
    for side in (0, 1):
        total, start = 0.0, 0
        for delta in deltas[side::2]:
            size = delta.shape[0]
            total = total + lax.dot_general(
                bf_ref[start : start + size], delta[...], (((0,), (0,)), ((), ())), preferred_element_type=F32)
            start += size
        for b in range(blocks):
            value = total[b * rows : (b + 1) * rows]
            if base:
                value = value + base[0][side, b, :rows].astype(F32)
            part_ref[side, b, :rows] = value.astype(BF)
            part_ref[side, b, rows:] = jnp.zeros((part_ref.shape[2] - rows, part_ref.shape[3]), BF)


def wgrad_part(normed_bf, deltas, first, owners, padded, base=None):
    features = normed_bf.shape[1]
    rows = sum(d.shape[0] for d in deltas[::2])
    width = deltas[0].shape[1]
    split = 2
    blocks = pl.BlockSpec((2, owners // split, padded, width), lambda i: (0, i, 0, 0))
    more = [] if base is None else [base]
    return pl.pallas_call(
        functools.partial(wgrad_kernel, len(deltas)),
        grid=(split,),
        in_specs=[pl.BlockSpec((rows, features // split), lambda i: (first // rows, i))]
        + [whole(d.shape) for d in deltas] + [blocks for _ in more],
        out_specs=blocks,
        out_shape=jax.ShapeDtypeStruct((2, owners, padded, width), BF),
        compiler_params=pltpu.CompilerParams(vmem_limit_bytes=58 * 2**20),
        cost_estimate=pl.CostEstimate(flops=2**20, bytes_accessed=2**16, transcendentals=0),
    )(normed_bf, *deltas, *more)


def place():
    dp = lax.axis_index("dp")
    x = lax.axis_index("rep") * 2 + lax.axis_index("tsec")
    return x, dp // 8, (dp // 2) % 4, dp % 2


def at_place(x, y, z, c):
    return {"tsec": x % 2, "dp": (y * 4 + z) * 2 + c, "rep": x // 2}


def tail_kernel(scale, part_ref, turned_ref, delta_ref, delta_far_ref, rank_ref, grad0_in, grad0_far_in, grad1_in,
                feature_out, dino_ref, siglip_ref,
                work, pair, far_y, far_z, far_y2, far_z2, far_x, stage, grad1_far,
                load_sem, pair_send, pair_recv, send_sem, recv_sem,
                feature_ref, grad0_ref, grad0_far_ref, grad1_ref, grad_sem, out_sem):
    x, y, z, c = place()
    t = x % 2
    sibling, partner = at_place(x, y, z, 1 - c), {"tsec": 1 - t}
    steps = [(h, j) for j in (2, 1, 3, 0) for h in (0, 1)]

    def line_of(h, j):
        return (y + j) % 4 if h == 0 else (z + j) % 4

    def load(h, j):
        line = line_of(h, j)
        src, dst = (r.at[0, line] if h == 0 else r.at[1, :, line] for r in (part_ref, work))
        return pltpu.make_async_copy(src, dst, load_sem.at[4 * h + j])

    for h, j in steps:
        load(h, j).start()
    grad_loads = [
        pltpu.make_async_copy(src, dst, grad_sem.at[i])
        for i, (src, dst) in enumerate(
            ((grad0_in, grad0_ref), (grad0_far_in, grad0_far_ref), (grad1_in, grad1_ref)))]
    def store(i):
        return pltpu.make_async_copy(feature_ref.at[tile_at(i)], feature_out.at[tile_at(i)], out_sem.at[i])

    lines = [[at_place(x, (y + j) % 4, z, c), at_place(x, y, (z + j) % 4, c), at_place((x + j) % 4, y, z, c)]
             for j in (1, 2, 3)]
    greet([sibling] + sum(lines, []))
    back = remote(grad1_in, grad1_far, send_sem.at[15], recv_sem.at[15], partner)
    back.start()
    rows = feature_ref.shape[1] // 32

    def add_products(h, j):
        delta = delta_ref if h == 0 else delta_far_ref
        line = line_of(h, j)
        features = pl.ds(pl.multiple_of(line * 8 * rows, 16), 8 * rows)
        new = jnp.dot(turned_ref[h, features], delta[...], preferred_element_type=F32)
        for b in range(8):
            at = (0, line, b // 2, b % 2) if h == 0 else (1, b // 2, line, b % 2)
            old = work[at + (slice(0, rows),)].astype(F32)
            work[at + (slice(0, rows),)] = (old + new[b * rows : (b + 1) * rows]).astype(BF)

    def pair_copy(h, j):
        line = line_of(h, j)
        src = work.at[0, line, :, 1 - c] if h == 0 else work.at[1, :, line, 1 - c]
        return remote(src, pair.at[h, j], pair_send.at[4 * h + j], pair_recv.at[4 * h + j], sibling)

    def line_copy(h, j):
        far = far_y if h == 0 else far_z
        device = at_place(x, (y + j) % 4, z, c) if h == 0 else at_place(x, y, (z + j) % 4, c)
        i = 3 * h + j - 1
        return remote(pair.at[h, j], far.at[j - 1], send_sem.at[i], recv_sem.at[i], device)

    def combine(h, j):
        pair_copy(h, j).wait_recv()
        line = line_of(h, j)

        @pl.loop(0, 4)
        def _(b):
            own = work[0, line, b, c] if h == 0 else work[1, b, line, c]
            pair[h, j, b] = (own.astype(F32) + pair[h, j, b].astype(F32)).astype(BF)

        if j:
            line_copy(h, j).start()

    lag = 2
    for i, (h, j) in enumerate(steps):
        load(h, j).wait()
        add_products(h, j)
        pair_copy(h, j).start()
        if i >= lag:
            combine(*steps[i - lag])
    for copy in grad_loads:
        copy.start()
    for h, j in steps[-lag:]:
        combine(h, j)

    for copy in grad_loads:
        copy.wait()

    count = grad0_ref.shape[0]
    starts = [(2 * s + side) * count for s in (0, 1) for side in (t, 1 - t)]

    @pl.loop(0, feature_ref.shape[0] // TILE)
    def _(i):
        total = 0.0
        for start, piece in zip(starts, (grad0_ref, grad0_far_ref, grad1_ref)):
            hit = hits(rank_ref[tile_at(i)], start, count)
            total = total + jnp.dot(hit, piece[...], preferred_element_type=F32)
        feature_ref[tile_at(i)] = total.astype(BF)

    for h, j in steps:
        pair_copy(h, j).wait_send()

    def cross_copy(h, j):
        far = far_z2 if h == 0 else far_y2
        b = (z + j) % 4 if h == 0 else (y + j) % 4
        device = at_place(x, y, b, c) if h == 0 else at_place(x, b, z, c)
        i = 6 + 3 * h + j - 1
        return remote(pair.at[h, 0, b], far.at[j - 1], send_sem.at[i], recv_sem.at[i], device)

    for h in (0, 1):
        far = far_y if h == 0 else far_z
        for j in (2, 1, 3):
            line_copy(h, j).wait()

        @pl.loop(0, 4)
        def _(b, h=h, far=far):
            pair[h, 0, b] = (pair[h, 0, b].astype(F32) + far[0, b].astype(F32)
                             + far[1, b].astype(F32) + far[2, b].astype(F32)).astype(BF)

        for j in (2, 1, 3):
            cross_copy(h, j).start()

    back.wait()

    @pl.loop(0, feature_ref.shape[0] // TILE)
    def _(i):
        hit = hits(rank_ref[tile_at(i)], starts[3], count)
        found = jnp.dot(hit, grad1_far[...], preferred_element_type=F32)
        feature_ref[tile_at(i)] = (feature_ref[tile_at(i)].astype(F32) + found).astype(BF)
        store(i).start()

    for h in (0, 1):
        far = far_z2 if h == 0 else far_y2
        for j in (2, 1, 3):
            cross_copy(h, j).wait()
        mine = pair[h, 0, z] if h == 0 else pair[h, 0, y]
        stage[h] = (mine.astype(F32) + far[0].astype(F32) + far[1].astype(F32) + far[2].astype(F32)).astype(BF)

    def x_copy(j):
        device = (x + j) % 4
        i = 12 + j - 1
        return remote(stage.at[(device + x) % 2], far_x.at[j - 1], send_sem.at[i], recv_sem.at[i],
                      at_place(device, y, z, c))

    for j in (2, 1, 3):
        x_copy(j).start()
    for j in (2, 1, 3):
        x_copy(j).wait()
    total = (stage[0].astype(F32) + far_x[0].astype(F32) + far_x[1].astype(F32) + far_x[2].astype(F32)) * scale
    @pl.loop(0, feature_ref.shape[0] // TILE)
    def _(i):
        store(i).wait()

    dino_ref[...] = total[:rows, : dino_ref.shape[1]]
    siglip_ref[...] = total[:rows, dino_ref.shape[1] :]


def finish(scale, part, turned, delta, delta_far, rank, grads, dino_cols):
    block = part.shape[-2:]
    count, features = grads[0].shape
    own_rows = features // 32
    return pl.pallas_call(
        functools.partial(tail_kernel, scale),
        out_shape=[
            jax.ShapeDtypeStruct((rank.shape[0], features), BF),
            jax.ShapeDtypeStruct((own_rows, dino_cols), F32),
            jax.ShapeDtypeStruct((own_rows, block[1] - dino_cols), F32)],
        in_specs=[HERE] + [VMEM] * 4 + [HERE] * 3,
        out_specs=[HERE] + [VMEM] * 2,
        scratch_shapes=[
            pltpu.VMEM((2, 4, 4, 2) + block, BF),
            pltpu.VMEM((2, 4, 4) + block, BF),
            pltpu.VMEM((3, 4) + block, BF),
            pltpu.VMEM((3, 4) + block, BF),
            pltpu.VMEM((3,) + block, BF),
            pltpu.VMEM((3,) + block, BF),
            pltpu.VMEM((3,) + block, BF),
            pltpu.VMEM((2,) + block, BF),
            pltpu.VMEM((count, features), BF),
            pltpu.SemaphoreType.DMA((8,)),
            pltpu.SemaphoreType.DMA((8,)),
            pltpu.SemaphoreType.DMA((8,)),
            pltpu.SemaphoreType.DMA((16,)),
            pltpu.SemaphoreType.DMA((16,)),
            pltpu.VMEM((rank.shape[0], features), BF),
        ]
        + [pltpu.VMEM((count, features), BF)] * 3
        + [pltpu.SemaphoreType.DMA((3,)), pltpu.SemaphoreType.DMA((rank.shape[0] // TILE,))],
        compiler_params=pltpu.CompilerParams(
            collective_id=0, has_side_effects=True, vmem_limit_bytes=60 * 2**20
        ),
        cost_estimate=pl.CostEstimate(flops=10**10, bytes_accessed=5 * 10**7, transcendentals=0),
    )(part, turned, delta, delta_far, rank, *grads)


def per_device(student, dino_feat, siglip_feat, dino_weight, siglip_weight, send_index, recv_index):
    n_dp = lax.axis_size("dp")
    groups = n_dp * lax.axis_size("rep")
    row_count = student.shape[0]
    capacity = 2 * row_count // groups
    dino_cols = dino_feat.shape[1]
    t = lax.axis_index("tsec")
    rep = lax.axis_index("rep")
    swap = [(0, 1), (1, 0)]
    mirrored = [
        [((tt ^ r) * n_dp + d) * 2 + r for d in range(n_dp) for r in range(2)] for tt in range(2)
    ]

    own_rows = student.shape[1] // n_dp
    padded = -(-own_rows // 16) * 16

    def place_in(chunk, code):
        start, size = CHUNKS[chunk]
        slot = code % capacity - start
        return jnp.where((slot >= 0) & (slot < size), code // capacity * size + slot, -1)

    def exchange(outbox, chunk):
        arrived = lax.all_to_all(
            outbox.reshape(groups, CHUNKS[chunk][1], -1),
            ("tsec", "dp", "rep"),
            split_axis=0,
            concat_axis=0,
            axis_index_groups=mirrored,
            tiled=True,
        )
        return arrived.reshape(outbox.shape)

    outbox = fill_outbox(
        place_in(0, send_index)[None, :], dino_feat, siglip_feat.T, groups * CHUNKS[0][1], send_index)
    inbox = exchange(outbox, 0)

    key = (recv_index % capacity) * groups + recv_index // capacity
    rank = jnp.sum((key[:, None] > key[None, :]).astype(I32), 1)
    ranks = jnp.arange(row_count, dtype=I32)
    code_at = jnp.sum(jnp.where(rank[None, :] == ranks[:, None], recv_index[None, :], 0), 1)
    quarter = row_count // 4

    def columns_of(whose):
        codes, order = [
            jnp.concatenate([
                lax.dynamic_slice(values, ((2 * stage + whose) * quarter,), (quarter,)) for stage in (0, 1)
            ])
            for values in (code_at, ranks)
        ]
        direct = ((codes // capacity) % 2 == rep).astype(I32)
        return jnp.stack([order, direct] + [place_in(c, codes) for c in range(len(CHUNKS))], 1)

    columns, columns_far = columns_of(t), columns_of(1 - t)
    weights = [dino_weight, siglip_weight.T]
    normed, normed_bf, inv_dev, out, out_far, *weights_far, outbox = forward(
        columns, rank[None, :], place_in(1, send_index)[None, :], student, dino_feat, siglip_feat.T, weights,
        groups * CHUNKS[1][1], outbox)
    weights = weights + weights_far
    inboxes = [inbox, exchange(outbox, 1)]

    turned = normed_bf[quarter:].T
    by_z = turned.reshape(4, 4, -1, quarter).transpose(1, 0, 2, 3).reshape(turned.shape)
    turned = jnp.stack([turned, by_z])
    bases, grads = [], []
    for stage in (0, 1):
        delta, delta_far, grad, *bases = handle_block(
            stage, columns, columns_far, inv_dev, inboxes[stage], out, out_far, normed, weights, bases)
        grads.append(grad)
        if stage == 0:
            grads.append(lax.ppermute(grad, "tsec", swap))
            part = wgrad_part(normed_bf, [delta, delta_far], 0, n_dp, padded)
            bases = bases + [part]

    part = part.reshape((2, 4, 4, 2) + part.shape[2:])
    grad_scale = 1.0 / math.sqrt(row_count * groups)
    return tuple(finish(grad_scale, part, turned, delta, delta_far, rank[:, None], grads, dino_cols))


def solution(mesh):
    placed = (
        P(("dp", "rep"), None),
        P(("dp", "rep"), "tsec"),
        P(("dp", "rep"), "tsec"),
        P(None, "tsec"),
        P(None, "tsec"),
        P(("dp", "rep")),
        P(("dp", "rep")),
    )
    return jax.shard_map(
        per_device,
        mesh=mesh,
        in_specs=placed,
        out_specs=(P(("dp", "rep"), None), P("dp", "tsec"), P("dp", "tsec")),
        check_vma=False,
    )
```
